512 devices in a mesh: db: 128 (over x, z, core), pb: 4 (over y).
Axes of the slice: x: 4, y: 4, z: 16, core: 2. Of those that a mesh axis runs over, the one named last changes fastest.
Arguments:
- keys: float32 [13312, 384], P(('db', 'pb')), may hold values from -6 to 6
- slab: float32 [12288, 384], P('db'), may hold values from -6 to 6
- neighbour_ids: int32 [13312, 2], P(('db', 'pb')), may hold values from 0 to 12287, as said below
- group_acts: bfloat16 [13312, 4, 896], P(('db', 'pb')), may hold values from -48 to 48
- table: bfloat16 [12288, 4, 896], P('db'), may hold values from -6 to 6
- norm_gain: float32 [896], replicated, may hold values from 0.1 to 1.9
- w_query: bfloat16 [896, 448], P('pb'), may hold values from -0.1875 to 0.1875
- w_key: bfloat16 [896, 448], P('pb'), may hold values from -0.1875 to 0.1875
- w_value: bfloat16 [896, 448], P('pb'), may hold values from -0.1875 to 0.1875
- w_out: bfloat16 [448, 896], P('pb'), may hold values from -0.25 to 0.25
Outputs:
- best: float32 [13312, 2], P(('db', 'pb'))
- encoded: bfloat16 [13312, 2, 4, 896], P(('db', 'pb'))
The draws below stay inside these ranges and needn't reach their ends.
Inputs may be any that keep to these rules, and one draw needn't show every extreme that they name: `neighbour_ids`: the owner of a neighbour is its id // 96. Among the 52 neighbours in the rows of one device (aligned blocks of 26 rows, devices in the order db+pb), no owner appears more than 2 times and some owner exactly 2 times; a group's two neighbours differ.
All inputs are finite; a program needn't handle non-finite values.
Results may differ from the reference program's by a relative error of at most 0.012.
Values may be sent and summed in bfloat16 or wider, within the bound.
No kernel may reach another device: no remote copies, remote signals or barrier semaphores. Data moves between devices by JAX's collectives and lax.ppermute only.
A program may use at most 64 MiB of HBM per device.

```python
import math
import jax
import jax.numpy as jnp
from jax import lax

KEY = 384
E = 896
HEADS = 7
HEAD_DIM = 64
NT = 4
CT = 4
DB_DEV = 96
QDEV = 26
QUERIES = 13312
DB_ROWS = 12288
HD = 448
N_DB = 128
N_PB = 4


def draw_neighbour_ids(key, part):
    blocks = N_DB * N_PB
    retrieval_positions = N_DB * 2
    base_key = jax.random.fold_in(key, 11)
    k_hot, k_base, k_force, shard_retrieval_count, k_order = jax.random.split(base_key, 5)
    frequent_entries = jax.random.permutation(k_hot, N_DB) < max(N_DB // 16, 1)
    rating_increment = jnp.where(jnp.repeat(frequent_entries, 2)[None, :], 2 ** 19, 0).astype(jnp.int32)
    reference_ranking_marks = jax.random.randint(k_base, (blocks, retrieval_positions), 0, 2 ** 20, dtype=jnp.int32)
    forced = jax.random.randint(k_force, (blocks,), 0, N_DB, dtype=jnp.int32)
    owner_of_slot = lax.iota(jnp.int32, retrieval_positions) // 2
    rating_shift = jnp.where(owner_of_slot[None, :] == forced[:, None], 2 ** 21, 0).astype(jnp.int32)
    lookup_match_rating = (reference_ranking_marks + rating_increment + rating_shift) * 512 + lax.iota(jnp.int32, retrieval_positions)[None, :]
    chosen = lax.top_k(lookup_match_rating, 2 * QDEV)[1].astype(jnp.int32)
    order_score = jax.random.randint(k_order, (blocks, 2 * QDEV), 0, 2 ** 20, dtype=jnp.int32) * 512 + lax.iota(jnp.int32, 2 * QDEV)[None, :]
    order = jnp.argsort(order_score, axis=1, stable=True).astype(jnp.int32)
    chosen = jnp.take_along_axis(chosen, order, axis=1)
    owner = chosen // 2
    half = chosen % 2
    local = half * (DB_DEV // 2) + jax.random.randint(shard_retrieval_count, (blocks, 2 * QDEV), 0, DB_DEV // 2, dtype=jnp.int32)
    return (owner * DB_DEV + local).reshape(QUERIES, 2).astype(jnp.int32)


def draw_group_acts(key, part):
    base_key = jax.random.fold_in(key, 7)
    k_main = jax.random.fold_in(base_key, 0)
    values = jnp.clip(jax.random.normal(k_main, (QUERIES, CT, E), jnp.float32), -6.0, 6.0)
    return values.astype(jnp.bfloat16)


def steps_of(own_key, dims, shards, low, largest):
    loudness, own = 1.0, jax.random.fold_in(own_key, 6)
    for axis_at, shards_of in shards:
        draws = jnp.exp(jax.random.uniform(jax.random.fold_in(own, axis_at), (shards_of,), jnp.float32, low / len(shards), largest / len(shards)))
        loudness = loudness * jnp.repeat(draws, dims[axis_at] // shards_of).reshape([-1 if axis == axis_at else 1 for axis in range(len(dims))])
    return loudness


def noise(rng, extent, scale, most, pieces=(), held_as=jnp.bfloat16):
    values = jax.random.normal(rng, extent, jnp.float32) * scale
    if len(pieces) > 0:
        values = steps_of(rng, extent, pieces, -0.22, 0.18) * values
    return jnp.clip(values, min=-most, max=most).astype(held_as)


def setup_inputs(seed: int = 0) -> dict:
    key_list = jax.random.split(jax.random.key(seed), 11)
    keys = noise(key_list[0], (QUERIES, KEY), 1.0, 6.0, ((0, 512),), jnp.float32)
    slab = noise(key_list[1], (DB_ROWS, KEY), 1.0, 6.0, ((0, 128),), jnp.float32)
    neighbour_ids = draw_neighbour_ids(jax.random.fold_in(key_list[10], 71), 0)
    group_acts = draw_group_acts(jax.random.fold_in(key_list[10], 71), 0)
    table = noise(key_list[4], (DB_ROWS, NT, E), 1.0, 6.0, ((0, 128),))
    norm_gain = jnp.clip(1.0 + 0.18 * jax.random.normal(key_list[5], (E,), jnp.float32), 0.1, 1.9)
    w_query = noise(key_list[6], (E, HD), E ** -0.5, 0.1875, ((0, 4),))
    w_key = noise(key_list[7], (E, HD), E ** -0.5, 0.1875, ((0, 4),))
    w_value = noise(key_list[8], (E, HD), E ** -0.5, 0.1875, ((0, 4),))
    w_out = noise(key_list[9], (HD, E), HD ** -0.5, 0.25, ((0, 4),))
    return {"keys": keys, "slab": slab, "neighbour_ids": neighbour_ids, "group_acts": group_acts, "table": table, "norm_gain": norm_gain, "w_query": w_query, "w_key": w_key, "w_value": w_value, "w_out": w_out}


def norm_rows(x, gain):
    values = x.astype(jnp.float32)
    square = lax.optimization_barrier(jnp.mean(values * values, axis=-1, keepdims=True))
    return (values * lax.rsqrt(square + 1e-06) * gain).astype(jnp.bfloat16)

def attend(x, keyed, value_weighted, w_query, w_out, gain):
    count = x.shape[0]
    rescaled_states = norm_rows(x, gain)
    query = jnp.dot(rescaled_states.reshape(count * NT, E), w_query, preferred_element_type=jnp.float32).astype(jnp.bfloat16)
    query = query.reshape(count, NT, HEADS, HEAD_DIM).astype(jnp.float32)
    khead = keyed.reshape(count, CT, HEADS, HEAD_DIM).astype(jnp.float32)
    vhead = value_weighted.reshape(count, CT, HEADS, HEAD_DIM).astype(jnp.float32)
    logits = jnp.einsum('snhd,schd->shnc', query, khead) / math.sqrt(HEAD_DIM)
    probs = jax.nn.softmax(logits, axis=-1).astype(jnp.bfloat16)
    mixed = jnp.einsum('shnc,schd->snhd', probs.astype(jnp.float32), vhead).astype(jnp.bfloat16)
    mixed = mixed.reshape(count * NT, HEADS * HEAD_DIM)
    result = x.reshape(count * NT, E).astype(jnp.float32) + jnp.dot(mixed, w_out, preferred_element_type=jnp.float32)
    return result.astype(jnp.bfloat16).reshape(count, NT, E)

def reference(keys, slab, neighbour_ids, group_acts, table, norm_gain, w_query, w_key, w_value, w_out):
    scale = 1.0 / math.sqrt(KEY)

    def score_block(block):
        lookup_match_rating = jnp.einsum('qk,rk->qr', block, slab, precision=lax.Precision.HIGHEST, preferred_element_type=jnp.float32) * scale
        return lax.top_k(lookup_match_rating, 2)[0]
    best = lax.map(score_block, keys.reshape(N_DB, QDEV * N_PB, KEY)).reshape(QUERIES, 2)

    def encode_block(inputs):
        ids_block, acts_block = inputs
        x = table[ids_block.reshape(2 * QDEV)]
        flat = acts_block.reshape(QDEV * CT, E)
        keyed = jnp.dot(flat, w_key, preferred_element_type=jnp.float32).astype(jnp.bfloat16).reshape(QDEV, CT, HD)
        value_weighted = jnp.dot(flat, w_value, preferred_element_type=jnp.float32).astype(jnp.bfloat16).reshape(QDEV, CT, HD)
        keyed = jnp.repeat(keyed, 2, axis=0)
        value_weighted = jnp.repeat(value_weighted, 2, axis=0)
        return attend(x, keyed, value_weighted, w_query, w_out, norm_gain).reshape(QDEV, 2, NT, E)
    encoded = lax.map(encode_block, (neighbour_ids.reshape(N_DB * N_PB, QDEV, 2), group_acts.reshape(N_DB * N_PB, QDEV, CT, E)))
    return (best, encoded.reshape(QUERIES, 2, NT, E))
```

```python
import jax
import jax.numpy as jnp
from jax import lax
from jax.experimental import pallas as pl
from jax.experimental.pallas import tpu as pltpu
from jax.sharding import Mesh
from jax.sharding import PartitionSpec as P

KEY = 384
E = 896
HEADS = 7
HSIZE = 64
HD = HEADS * HSIZE
NT = 4
CT = 4
ROWS = 96
GROUPS = 26
PAIRS = 2 * GROUPS
RING = 8
PIECE = 112
SLAB_ROWS = 12
SERVERS = 64
SLOTS = 16
KEYPAD = 32
WIDE = E + 128
CUT = 64
LOW = -3.0e38
SPLIT = ("x", "zh", "zl", "core", "pb")
DB = ("x", "zh", "zl", "core")
NEAR = ("pb", "x", "zl", "core")
BF = jnp.bfloat16
F32 = jnp.float32


def best_two(hi, lo):
    count = hi.shape[0]
    while count > 1:
        half = count // 2
        h1, h2, l1, l2 = hi[:half], hi[half:count], lo[:half], lo[half:count]
        hi, lo = jnp.maximum(h1, h2), jnp.maximum(jnp.minimum(h1, h2), jnp.maximum(l1, l2))
        count = half
    return hi, lo


def serve_kernel(code, keys, *refs):
    pieces, out, held, slab = refs[: RING + 1], refs[RING + 1], refs[RING + 2], refs[RING + 3]
    at = 0
    for piece in pieces:
        rows = piece.shape[0]
        held[at : at + rows, :] = piece[...]
        at += rows
    for k in range(RING):
        for part in range(2):
            slab[(2 * k + part) * 16 : (2 * k + part + 1) * 16, :] = held[
                k * PIECE + ROWS : (k + 1) * PIECE, part * KEY : (part + 1) * KEY
            ]
    step = 256
    for i in range(SERVERS * SLOTS // step):
        label = lax.broadcasted_iota(jnp.int32, (step, RING * PIECE), 1)
        pick = (code[i * step : (i + 1) * step, :] == label).astype(F32).astype(BF)
        found = jnp.dot(pick, held[...], preferred_element_type=F32).astype(BF)
        n = step // SLOTS
        out[i * n : (i + 1) * n, :, :E] = found.reshape(n, SLOTS, E)
    queries = SERVERS * KEYPAD
    wide = 512
    n = wide // KEYPAD
    for i in range(queries // wide):
        block = keys[i * n : (i + 1) * n].reshape(wide, KEY)
        rating = lax.dot_general(
            slab[...], block, (((1,), (1,)), ((), ())), preferred_element_type=F32
        ) * (KEY**-0.5)
        row = lax.broadcasted_iota(jnp.int32, rating.shape, 0)
        rating = jnp.where(lax.rem(row, 16) < SLAB_ROWS, rating, LOW)
        h1, h2 = rating[:128], rating[128:]
        hi, lo = best_two(jnp.maximum(h1, h2), jnp.minimum(h1, h2))
        hi_a = hi.astype(BF).astype(F32)
        lo_a = lo.astype(BF).astype(F32)
        line = lax.broadcasted_iota(jnp.int32, (16, wide), 0)
        parts = jnp.where(
            line == 0,
            hi_a,
            jnp.where(line == 1, hi - hi_a, jnp.where(line == 2, lo_a, jnp.where(line == 3, lo - lo_a, 0.0))),
        ).astype(BF)
        for half in range(2):
            unit = (
                lax.broadcasted_iota(jnp.int32, (16, 128), 0) + 4 * half
                == lax.broadcasted_iota(jnp.int32, (16, 128), 1)
            ).astype(F32).astype(BF)
            turned = lax.dot_general(
                parts, unit, (((0,), (0,)), ((), ())), preferred_element_type=F32
            ).reshape(n, 2, 16, 128)
            if half == 0:
                total = turned[:, 0]
            else:
                total = total + turned[:, 1]
        out[i * n : (i + 1) * n, :, E:] = total.astype(BF)


def layer_kernel(place, got, keyed, valued, w_query, w_out, gain, best, encoded):
    label = lax.broadcasted_iota(jnp.int32, (PAIRS * NT, SERVERS * SLOTS), 1)
    pick = (place[...] == label).astype(F32).astype(BF)
    rows = got[:, :, :E].reshape(SERVERS * SLOTS, E)
    x = jnp.dot(pick, rows, preferred_element_type=F32)
    square = jnp.mean(x * x, axis=-1, keepdims=True)
    normed = (x * lax.rsqrt(square + 1e-06) * gain[...]).astype(BF)
    query = jnp.dot(normed, w_query[:, :HD], preferred_element_type=F32).astype(BF)
    query = query.astype(F32)
    k_all = keyed[...]
    v_all = valued[...].astype(F32)
    head = lax.broadcasted_iota(jnp.int32, (1, HD), 1) // HSIZE
    mine = (
        lax.broadcasted_iota(jnp.int32, (PAIRS * NT, GROUPS * CT), 0) // (2 * NT)
        == lax.broadcasted_iota(jnp.int32, (PAIRS * NT, GROUPS * CT), 1) // CT
    )
    mixed = jnp.zeros((PAIRS * NT, HD), F32)
    for h in range(HEADS):
        q_h = jnp.where(head == h, query, 0.0).astype(BF)
        v_h = jnp.where(head == h, v_all, 0.0).astype(BF)
        logits = lax.dot_general(
            q_h, k_all, (((1,), (1,)), ((), ())), preferred_element_type=F32
        ) * (HSIZE**-0.5)
        logits = jnp.where(mine, logits, LOW)
        top = jnp.max(logits, axis=-1, keepdims=True)
        e = jnp.exp(logits - top)
        probs = (e / jnp.sum(e, axis=-1, keepdims=True)).astype(BF)
        mixed = mixed + jnp.dot(probs, v_h, preferred_element_type=F32)
    result = x + jnp.dot(mixed.astype(BF), w_out[...], preferred_element_type=F32)
    encoded[...] = result.astype(BF)
    c = got[:, :, E:].astype(F32)
    c = c + pltpu.roll(c, 127, 2)
    hi, lo = best_two(c, pltpu.roll(c, 126, 2))
    hi, lo = hi[0], lo[0]
    for half in range(2):
        n = min(16, GROUPS - 16 * half)
        best[16 * half : 16 * half + n, 0:1] = hi[:n, 4 * half : 4 * half + 1]
        best[16 * half : 16 * half + n, 1:2] = lo[:n, 4 * half : 4 * half + 1]


def vmem(count):
    return [pl.BlockSpec(memory_space=pltpu.VMEM)] * count


def ring_moved(piece, step):
    return lax.ppermute(piece, "zh", [(i, (i + step) % RING) for i in range(RING)])


def per_device(keys, slab, neighbour_ids, group_acts, table, norm_gain, w_query, w_key, w_value, w_out):
    y = lax.axis_index("pb")
    zh = lax.axis_index("zh")
    token = lax.dynamic_index_in_dim(table, y, axis=1, keepdims=False)
    quarter = lax.dynamic_slice_in_dim(slab, y * 2 * SLAB_ROWS, 2 * SLAB_ROWS, 0).astype(BF)
    quarter = jnp.concatenate([quarter[:SLAB_ROWS], quarter[SLAB_ROWS:]], axis=1)
    quarter = jnp.pad(quarter, ((0, PIECE - ROWS - SLAB_ROWS), (0, E - 2 * KEY)))
    piece = jnp.concatenate([token, quarter], axis=0)
    right = [piece]
    left = [piece]
    for _ in range(3):
        right.append(ring_moved(right[-1], 1))
        left.append(ring_moved(left[-1], -1))
    far_a = ring_moved(right[3][:CUT], 1)
    far_b = ring_moved(left[3][CUT:], -1)
    pieces = [*right, far_a, far_b, left[3], left[2], left[1]]
    packed = jnp.concatenate(
        [
            jnp.concatenate([w_query, w_key], axis=1),
            jnp.concatenate([w_value[: ROWS + 16], w_value[ROWS + 16 :]], axis=1),
            w_out,
        ],
        axis=0,
    )
    whole = lax.all_gather(packed, "pb", axis=0, tiled=False)
    part = w_query.shape[0]
    w_qk = whole[:, :part].reshape(E, 2 * HD)
    w_v = whole[:, part : part + part // 2]
    w_v = jnp.concatenate([w_v[:, :, :HD], w_v[:, :, HD:]], axis=1).reshape(E, HD)
    w_o = whole[:, part + part // 2 :].reshape(HD, E)
    flat = neighbour_ids.T.reshape(PAIRS)
    owner = lax.div(flat, ROWS)
    local = flat - owner * ROWS
    at = lax.iota(jnp.int32, PAIRS)
    rank = jnp.max(
        jnp.where((owner[:, None] == owner[None, :]) & (at[:, None] > at[None, :]), 1, 0), axis=1
    )
    server = ((owner >> 5) << 2) | (owner & 3)
    code = server * SLOTS + ((owner >> 2) & 7) * 2 + rank
    marks = jnp.sum(
        jnp.where(code[None, :] == lax.iota(jnp.int32, 16 * SLOTS)[:, None], local[None, :] + 1, 0), axis=1
    )
    marks = marks.astype(BF).reshape(16, SLOTS)
    place = code.reshape(2, GROUPS).T.reshape(GROUPS, 2, 1) + lax.iota(jnp.int32, NT) * (16 * SLOTS)
    place = place.reshape(PAIRS * NT, 1)
    sent = jnp.pad(keys.astype(BF), ((0, KEYPAD - GROUPS), (0, 0)))
    marks = jnp.pad(marks[:, None, :], ((0, 0), (GROUPS, KEYPAD - GROUPS - 1), (0, KEY - SLOTS)))
    sent = sent[None] + marks
    sent = jnp.broadcast_to(sent[None], (4, 16, KEYPAD, KEY)).reshape(SERVERS, KEYPAD, KEY)
    asked = lax.all_to_all(sent, NEAR, split_axis=0, concat_axis=0, tiled=True)
    wanted = asked[:, GROUPS, :SLOTS].astype(jnp.int32)
    away = jnp.bitwise_and(zh - lax.iota(jnp.int32, SLOTS) // 2 + RING, RING - 1)
    wanted = jnp.where(wanted > 0, away[None, :] * PIECE + wanted - 1, -1).reshape(SERVERS * SLOTS, 1)
    served = pl.pallas_call(
        serve_kernel,
        out_shape=jax.ShapeDtypeStruct((SERVERS, SLOTS, WIDE), BF),
        in_specs=vmem(2 + RING + 1),
        out_specs=pl.BlockSpec(memory_space=pltpu.VMEM),
        scratch_shapes=[pltpu.VMEM((RING * PIECE, E), BF), pltpu.VMEM((RING * 32, KEY), BF)],
        compiler_params=pltpu.CompilerParams(vmem_limit_bytes=32 * 2**20),
    )(wanted, asked, *pieces)
    got = lax.all_to_all(served, NEAR, split_axis=0, concat_axis=0, tiled=True)
    acts = group_acts.reshape(GROUPS * CT, E)
    keyed = jnp.dot(acts, w_qk[:, HD:], preferred_element_type=F32).astype(BF)
    valued = jnp.dot(acts, w_v, preferred_element_type=F32).astype(BF)
    best, encoded = pl.pallas_call(
        layer_kernel,
        out_shape=(
            jax.ShapeDtypeStruct((GROUPS, 2), F32),
            jax.ShapeDtypeStruct((PAIRS * NT, E), BF),
        ),
        in_specs=vmem(7),
        out_specs=tuple(vmem(2)),
        compiler_params=pltpu.CompilerParams(vmem_limit_bytes=32 * 2**20),
    )(place, got, keyed, valued, w_qk, w_o, norm_gain.reshape(1, E))
    return best, encoded.reshape(GROUPS, 2, NT, E)


def solution(mesh):
    split = Mesh(mesh.devices.reshape(4, RING, 2, 2, 4), SPLIT)
    return jax.shard_map(
        per_device,
        mesh=split,
        in_specs=(
            P(SPLIT, None),
            P(DB, None),
            P(SPLIT, None),
            P(SPLIT, None, None),
            P(DB, None, None),
            P(),
            P("pb", None),
            P("pb", None),
            P("pb", None),
            P("pb", None),
        ),
        out_specs=(P(SPLIT, None), P(SPLIT, None, None, None)),
        check_vma=False,
    )
```

```python
import jax
import jax.numpy as jnp
from jax import lax
from jax.experimental import pallas as pl
from jax.experimental.pallas import tpu as pltpu
from jax.sharding import Mesh
from jax.sharding import PartitionSpec as P

KEY = 384
E = 896
HEADS = 7
HSIZE = 64
HD = HEADS * HSIZE
NT = 4
CT = 4
ROWS = 96
GROUPS = 26
PAIRS = 2 * GROUPS
RING = 8
SLAB_ROWS = 24
PIECE = ROWS + SLAB_ROWS
PLANE = 32
SERVERS = 2 * PLANE
SLOTS = 16
KEYPAD = 32
WIDE = E + 128
CUT = 64
LOW = -1.0e38
SPLIT = ("x", "zh", "zl", "core", "pb")
DB = ("x", "zh", "zl", "core")
FLAT = ("pb", "x", "core")
NEAR = ("zl", *FLAT)
BF = jnp.bfloat16
F32 = jnp.float32


def best_two(hi, lo):
    count = hi.shape[0]
    while count > 1:
        half = count // 2
        h1, h2, l1, l2 = hi[:half], hi[half:count], lo[:half], lo[half:count]
        hi, lo = jnp.maximum(h1, h2), jnp.maximum(jnp.minimum(h1, h2), jnp.maximum(l1, l2))
        count = half
    return hi, lo


def serve_kernel(parity, code, keys, *refs):
    *pieces, far_a, far_b, out, held, slab = refs
    for k in range(RING):
        if k == RING // 2:
            held[k * ROWS : k * ROWS + CUT, :] = far_a[...]
            held[k * ROWS + CUT : (k + 1) * ROWS, :] = far_b[: ROWS - CUT, :]
            extra = far_b[ROWS - CUT :, :]
        else:
            piece = pieces[k if k < RING // 2 else k - 1]
            held[k * ROWS : (k + 1) * ROWS, :] = piece[:ROWS, :]
            extra = piece[ROWS:, :]
        for part in range(2):
            at = (2 * k + part) * SLAB_ROWS
            slab[at : at + SLAB_ROWS, :] = extra[:, part * KEY : (part + 1) * KEY].astype(F32)
    step = 256
    for i in range(SERVERS * SLOTS // step):
        label = lax.broadcasted_iota(jnp.int32, (step, RING * ROWS), 1)
        pick = (code[i * step : (i + 1) * step, :] == label).astype(F32).astype(BF)
        found = jnp.dot(pick, held[...], preferred_element_type=F32).astype(BF)
        n = step // SLOTS
        out[i * n : (i + 1) * n, :, :E] = found.reshape(n, SLOTS, E)
    wide = 512
    n = wide // KEYPAD
    rows = slab[...].astype(BF)
    mine = parity[...]
    for i in range(PLANE * KEYPAD // wide):
        block = keys[i * n : (i + 1) * n].reshape(wide, KEY)
        rating = lax.dot_general(
            rows, block, (((1,), (1,)), ((), ())), preferred_element_type=F32
        ) * (KEY**-0.5)
        h1, h2, h3 = rating[:128], rating[128:256], rating[256:]
        hi, lo = jnp.maximum(h1, h2), jnp.minimum(h1, h2)
        hi, lo = jnp.maximum(hi, h3), jnp.maximum(lo, jnp.minimum(hi, h3))
        hi, lo = best_two(hi, lo)
        hi_a = hi.astype(BF).astype(F32)
        lo_a = lo.astype(BF).astype(F32)
        line = lax.broadcasted_iota(jnp.int32, (16, wide), 0)
        parts = jnp.where(
            line == 0,
            hi_a,
            jnp.where(line == 1, hi - hi_a, jnp.where(line == 2, lo_a, jnp.where(line == 3, lo - lo_a, 0.0))),
        ).astype(BF)
        for half in range(2):
            unit = (
                lax.broadcasted_iota(jnp.int32, (16, 128), 0) + 4 * half
                == lax.broadcasted_iota(jnp.int32, (16, 128), 1)
            ).astype(F32).astype(BF)
            turned = lax.dot_general(
                parts, unit, (((0,), (0,)), ((), ())), preferred_element_type=F32
            ).reshape(n, 2, 16, 128)
            if half == 0:
                total = turned[:, 0]
            else:
                total = total + turned[:, 1]
        lane = lax.broadcasted_iota(jnp.int32, (1, 1, 128), 2)
        none = jnp.where(lax.rem(lane, 2) == 0, LOW, 0.0)
        for z in range(2):
            at = z * PLANE + i * n
            out[at : at + n, :, E:] = jnp.where(mine == z, total, none).astype(BF)


def layer_kernel(place, got, keyed, valued, w_query, w_out, gain, best, encoded):
    label = lax.broadcasted_iota(jnp.int32, (PAIRS * NT, SERVERS * SLOTS), 1)
    pick = (place[...] == label).astype(F32).astype(BF)
    rows = got[:, :, :E].reshape(SERVERS * SLOTS, E)
    x = jnp.dot(pick, rows, preferred_element_type=F32)
    square = jnp.mean(x * x, axis=-1, keepdims=True)
    normed = (x * lax.rsqrt(square + 1e-06) * gain[...]).astype(BF)
    query = jnp.dot(normed, w_query[:, :HD], preferred_element_type=F32).astype(BF)
    query = query.astype(F32)
    k_all = keyed[...]
    v_all = valued[...].astype(F32)
    head = lax.broadcasted_iota(jnp.int32, (1, HD), 1) // HSIZE
    mine = (
        lax.broadcasted_iota(jnp.int32, (PAIRS * NT, GROUPS * CT), 0) // (2 * NT)
        == lax.broadcasted_iota(jnp.int32, (PAIRS * NT, GROUPS * CT), 1) // CT
    )
    mixed = jnp.zeros((PAIRS * NT, HD), F32)
    for h in range(HEADS):
        q_h = jnp.where(head == h, query, 0.0).astype(BF)
        v_h = jnp.where(head == h, v_all, 0.0).astype(BF)
        logits = lax.dot_general(
            q_h, k_all, (((1,), (1,)), ((), ())), preferred_element_type=F32
        ) * (HSIZE**-0.5)
        logits = jnp.where(mine, logits, LOW)
        top = jnp.max(logits, axis=-1, keepdims=True)
        e = jnp.exp(logits - top)
        probs = (e / jnp.sum(e, axis=-1, keepdims=True)).astype(BF)
        mixed = mixed + jnp.dot(probs, v_h, preferred_element_type=F32)
    result = x + jnp.dot(mixed.astype(BF), w_out[...], preferred_element_type=F32)
    encoded[...] = result.astype(BF)
    c = got[:, :, E:].astype(F32)
    c = c + pltpu.roll(c, 127, 2)
    hi, lo = best_two(c, pltpu.roll(c, 126, 2))
    hi, lo = hi[0], lo[0]
    for half in range(2):
        n = min(16, GROUPS - 16 * half)
        best[16 * half : 16 * half + n, 0:1] = hi[:n, 4 * half : 4 * half + 1]
        best[16 * half : 16 * half + n, 1:2] = lo[:n, 4 * half : 4 * half + 1]


def vmem(count):
    return [pl.BlockSpec(memory_space=pltpu.VMEM)] * count


def ring_moved(piece, step):
    return lax.ppermute(piece, "zh", [(i, (i + step) % RING) for i in range(RING)])


def per_device(keys, slab, neighbour_ids, group_acts, table, norm_gain, w_query, w_key, w_value, w_out):
    y = lax.axis_index("pb")
    zh = lax.axis_index("zh")
    zl = lax.axis_index("zl")
    packed = jnp.concatenate(
        [
            jnp.concatenate([w_query, w_key], axis=1),
            jnp.concatenate([w_value[: ROWS + 16], w_value[ROWS + 16 :]], axis=1),
            w_out,
        ],
        axis=0,
    )
    whole = lax.all_gather(packed, "pb", axis=0, tiled=False)
    part = w_query.shape[0]
    w_qk = whole[:, :part].reshape(E, 2 * HD)
    w_v = whole[:, part : part + part // 2]
    w_v = jnp.concatenate([w_v[:, :, :HD], w_v[:, :, HD:]], axis=1).reshape(E, HD)
    w_o = whole[:, part + part // 2 :].reshape(HD, E)
    acts = group_acts.reshape(GROUPS * CT, E)
    keyed = jnp.dot(acts, w_qk[:, HD:], preferred_element_type=F32).astype(BF)
    valued = jnp.dot(acts, w_v, preferred_element_type=F32).astype(BF)
    flat = neighbour_ids.T.reshape(PAIRS)
    owner = lax.div(flat, ROWS)
    local = flat - owner * ROWS
    at = lax.iota(jnp.int32, PAIRS)
    rank = jnp.max(
        jnp.where((owner[:, None] == owner[None, :]) & (at[:, None] > at[None, :]), 1, 0), axis=1
    )
    column = ((owner >> 5) << 1) | (owner & 1)
    code = ((owner >> 1) & 1) * 128 + column * SLOTS + ((owner >> 2) & 7) * 2 + rank
    place = (code >> 7) * (PLANE * SLOTS) + (code & 127)
    place = place.reshape(2, GROUPS).T.reshape(GROUPS, 2, 1) + lax.iota(jnp.int32, NT) * 128
    place = place.reshape(PAIRS * NT, 1)
    flip = code ^ (zl * 128)
    marks = jnp.sum(
        jnp.where(flip[None, :] == lax.iota(jnp.int32, 256)[:, None], local[None, :] + 1, 0), axis=1
    )
    marks = marks.astype(BF)
    quarter = lax.dynamic_slice_in_dim(slab, y * SLAB_ROWS, SLAB_ROWS, 0).astype(BF)
    other = jnp.pad(marks[None, 128:], ((0, KEYPAD - SLAB_ROWS - 1), (0, KEY - 128)))
    pair = jnp.concatenate([quarter, other], axis=0)
    pair = lax.ppermute(pair, "zl", [(0, 1), (1, 0)])
    token = lax.dynamic_index_in_dim(table, y, axis=1, keepdims=False)
    both = jnp.concatenate([quarter, pair[:SLAB_ROWS]], axis=1)
    both = jnp.pad(both, ((0, 0), (0, E - 2 * KEY)))
    piece = jnp.concatenate([token, both], axis=0)
    right = [piece]
    left = [piece]
    for _ in range(3):
        right.append(ring_moved(right[-1], 1))
        left.append(ring_moved(left[-1], -1))
    far_a = ring_moved(right[3][:CUT], 1)
    far_b = ring_moved(left[3][CUT:], -1)
    pieces = [*right, left[3], left[2], left[1], far_a, far_b]
    sent = jnp.pad(keys.astype(BF), ((0, KEYPAD - GROUPS), (0, 0)))
    asks = jnp.stack([marks[:128].reshape(8, SLOTS), pair[SLAB_ROWS, :128].reshape(8, SLOTS)], axis=1)
    asks = jnp.pad(asks, ((0, 0), (GROUPS, KEYPAD - GROUPS - 2), (0, KEY - SLOTS)))
    sent = sent[None] + asks
    sent = jnp.broadcast_to(sent[None], (4, 8, KEYPAD, KEY)).reshape(PLANE, KEYPAD, KEY)
    asked = lax.all_to_all(sent, FLAT, split_axis=0, concat_axis=0, tiled=True)
    wanted = asked[:, GROUPS : GROUPS + 2, :SLOTS].astype(jnp.int32)
    wanted = jnp.where(zl == 0, jnp.stack([wanted[:, 0], wanted[:, 1]]), jnp.stack([wanted[:, 1], wanted[:, 0]]))
    away = jnp.bitwise_and(zh - lax.iota(jnp.int32, SLOTS) // 2 + RING, RING - 1)
    wanted = jnp.where(wanted > 0, away * ROWS + wanted - 1, -1).reshape(SERVERS * SLOTS, 1)
    wanted, keyed, valued = lax.optimization_barrier((wanted, keyed, valued))
    parity = jnp.full((1, 1, 128), zl, jnp.int32)
    served = pl.pallas_call(
        serve_kernel,
        out_shape=jax.ShapeDtypeStruct((SERVERS, SLOTS, WIDE), BF),
        in_specs=vmem(3 + RING + 1),
        out_specs=pl.BlockSpec(memory_space=pltpu.VMEM),
        scratch_shapes=[pltpu.VMEM((RING * ROWS, E), BF), pltpu.VMEM((RING * 2 * SLAB_ROWS, KEY), F32)],
        compiler_params=pltpu.CompilerParams(vmem_limit_bytes=32 * 2**20),
    )(parity, wanted, asked, *pieces)
    got = lax.all_to_all(served, NEAR, split_axis=0, concat_axis=0, tiled=True)
    best, encoded = pl.pallas_call(
        layer_kernel,
        out_shape=(
            jax.ShapeDtypeStruct((GROUPS, 2), F32),
            jax.ShapeDtypeStruct((PAIRS * NT, E), BF),
        ),
        in_specs=vmem(7),
        out_specs=tuple(vmem(2)),
        compiler_params=pltpu.CompilerParams(vmem_limit_bytes=32 * 2**20),
    )(place, got, keyed, valued, w_qk, w_o, norm_gain.reshape(1, E))
    return best, encoded.reshape(GROUPS, 2, NT, E)


def solution(mesh):
    split = Mesh(mesh.devices.reshape(4, RING, 2, 2, 4), SPLIT)
    return jax.shard_map(
        per_device,
        mesh=split,
        in_specs=(
            P(SPLIT, None),
            P(DB, None),
            P(SPLIT, None),
            P(SPLIT, None, None),
            P(DB, None, None),
            P(),
            P("pb", None),
            P("pb", None),
            P("pb", None),
            P("pb", None),
        ),
        out_specs=(P(SPLIT, None), P(SPLIT, None, None, None)),
        check_vma=False,
    )
```

```python
import jax
import jax.numpy as jnp
from jax import lax
from jax.experimental import pallas as pl
from jax.experimental.pallas import tpu as pltpu
from jax.sharding import Mesh
from jax.sharding import PartitionSpec as P

KEY = 384
E = 896
HEADS = 7
HSIZE = 64
HD = HEADS * HSIZE
NT = 4
CT = 4
ROWS = 96
GROUPS = 26
PAIRS = 2 * GROUPS
RING = 8
SLAB_ROWS = 24
PIECE = ROWS + SLAB_ROWS
PLANE = 32
SERVERS = 2 * PLANE
SLOTS = 16
KEYPAD = 32
WIDE = E + 128
CUT = 64
LIMIT = 52 * 2**20
SERVE_LIMIT = 52 * 2**20
LOW = -1.0e38
SPLIT = ("x", "zh", "zl", "core", "pb")
DB = ("x", "zh", "zl", "core")
FLAT = ("pb", "x", "core")
NEAR = ("zl", *FLAT)
BF = jnp.bfloat16
F32 = jnp.float32


def best_two(hi, lo):
    count = hi.shape[0]
    while count > 1:
        half = count // 2
        h1, h2, l1, l2 = hi[:half], hi[half:count], lo[:half], lo[half:count]
        hi, lo = jnp.maximum(h1, h2), jnp.maximum(jnp.minimum(h1, h2), jnp.maximum(l1, l2))
        count = half
    return hi, lo


def serve_kernel(parity, tick, code, keys, *refs):
    *pieces, far_a, far_b, sent, held, slab, out, sems = refs
    for k in range(RING):
        if k == RING // 2:
            held[k * ROWS : k * ROWS + CUT, :] = far_a[...]
            held[k * ROWS + CUT : (k + 1) * ROWS, :] = far_b[: ROWS - CUT, :]
            extra = far_b[ROWS - CUT :, :]
        else:
            piece = pieces[k if k < RING // 2 else k - 1]
            held[k * ROWS : (k + 1) * ROWS, :] = piece[:ROWS, :]
            extra = piece[ROWS:, :]
        for part in range(2):
            at = (2 * k + part) * SLAB_ROWS
            slab[at : at + SLAB_ROWS, :] = extra[:, part * KEY : (part + 1) * KEY].astype(F32)
    wide = 512
    n = wide // KEYPAD
    rows = slab[...].astype(BF)
    mine = parity[...]
    for i in range(PLANE * KEYPAD // wide):
        block = keys[i * n : (i + 1) * n].reshape(wide, KEY)
        rating = lax.dot_general(
            rows, block, (((1,), (1,)), ((), ())), preferred_element_type=F32
        ) * (KEY**-0.5)
        h1, h2, h3 = rating[:128], rating[128:256], rating[256:]
        hi, lo = jnp.maximum(h1, h2), jnp.minimum(h1, h2)
        hi, lo = jnp.maximum(hi, h3), jnp.maximum(lo, jnp.minimum(hi, h3))
        hi, lo = best_two(hi, lo)
        hi_a = hi.astype(BF).astype(F32)
        lo_a = lo.astype(BF).astype(F32)
        line = lax.broadcasted_iota(jnp.int32, (16, wide), 0)
        parts = jnp.where(
            line == 0,
            hi_a,
            jnp.where(line == 1, hi - hi_a, jnp.where(line == 2, lo_a, jnp.where(line == 3, lo - lo_a, 0.0))),
        ).astype(BF)
        for half in range(2):
            unit = (
                lax.broadcasted_iota(jnp.int32, (16, 128), 0) + 4 * half
                == lax.broadcasted_iota(jnp.int32, (16, 128), 1)
            ).astype(F32).astype(BF)
            turned = lax.dot_general(
                parts, unit, (((0,), (0,)), ((), ())), preferred_element_type=F32
            ).reshape(n, 2, 16, 128)
            if half == 0:
                total = turned[:, 0]
            else:
                total = total + turned[:, 1]
        lane = lax.broadcasted_iota(jnp.int32, (1, 1, 128), 2)
        none = jnp.where(lax.rem(lane, 2) == 0, LOW, 0.0)
        for z in range(2):
            at = z * PLANE + i * n
            out[at : at + n, :, E:] = jnp.where(mine == z, total, none).astype(BF)
    step = 256
    n = step // SLOTS
    copies = []
    for i in range(SERVERS * SLOTS // step):
        label = lax.broadcasted_iota(jnp.int32, (step, RING * ROWS), 1)
        pick = (code[i * step : (i + 1) * step, :] == label).astype(F32).astype(BF)
        found = jnp.dot(pick, held[...], preferred_element_type=F32).astype(BF)
        out[i * n : (i + 1) * n, :, :E] = found.reshape(n, SLOTS, E)
        block = pl.ds(i * n, n)
        copies.append(pltpu.make_async_copy(out.at[block], sent.at[block], sems.at[i]))
        copies[-1].start()
    for copy in copies:
        copy.wait()


def layer_kernel(place, got, keyed, valued, whole, gain, best, encoded, w_query, w_out, sems):
    copies = []
    part = E // 4
    for b in range(4):
        copies.append(
            pltpu.make_async_copy(
                whole.at[b, pl.ds(0, part)], w_query.at[pl.ds(b * part, part)], sems.at[b]
            )
        )
    for b in range(4):
        copies.append(
            pltpu.make_async_copy(
                whole.at[b, pl.ds(part + part // 2, part // 2)],
                w_out.at[pl.ds(b * part // 2, part // 2)],
                sems.at[4 + b],
            )
        )
    for copy in copies:
        copy.start()
    label = lax.broadcasted_iota(jnp.int32, (PAIRS * NT, SERVERS * SLOTS), 1)
    pick = (place[...] == label).astype(F32).astype(BF)
    rows = got[:, :, :E].reshape(SERVERS * SLOTS, E)
    x = jnp.dot(pick, rows, preferred_element_type=F32)
    square = jnp.mean(x * x, axis=-1, keepdims=True)
    normed = (x * lax.rsqrt(square + 1e-06) * gain[...]).astype(BF)
    for copy in copies:
        copy.wait()
    query = jnp.dot(normed, w_query[:, :HD], preferred_element_type=F32).astype(BF)
    query = query.astype(F32)
    k_all = keyed[...]
    v_all = valued[...].astype(F32)
    head = lax.broadcasted_iota(jnp.int32, (1, HD), 1) // HSIZE
    mine = (
        lax.broadcasted_iota(jnp.int32, (PAIRS * NT, GROUPS * CT), 0) // (2 * NT)
        == lax.broadcasted_iota(jnp.int32, (PAIRS * NT, GROUPS * CT), 1) // CT
    )
    mixed = jnp.zeros((PAIRS * NT, HD), F32)
    for h in range(HEADS):
        q_h = jnp.where(head == h, query, 0.0).astype(BF)
        v_h = jnp.where(head == h, v_all, 0.0).astype(BF)
        logits = lax.dot_general(
            q_h, k_all, (((1,), (1,)), ((), ())), preferred_element_type=F32
        ) * (HSIZE**-0.5)
        logits = jnp.where(mine, logits, LOW)
        top = jnp.max(logits, axis=-1, keepdims=True)
        e = jnp.exp(logits - top)
        probs = (e / jnp.sum(e, axis=-1, keepdims=True)).astype(BF)
        mixed = mixed + jnp.dot(probs, v_h, preferred_element_type=F32)
    result = x + jnp.dot(mixed.astype(BF), w_out[...], preferred_element_type=F32)
    encoded[...] = result.astype(BF).reshape(GROUPS, 2, NT, E)
    c = got[:, :, E:].astype(F32)
    c = c + pltpu.roll(c, 127, 2)
    hi, lo = best_two(c, pltpu.roll(c, 126, 2))
    line = lax.broadcasted_iota(jnp.int32, (16, 128), 0)
    lane = lax.broadcasted_iota(jnp.int32, (16, 128), 1)
    for k, value in enumerate((hi[0], lo[0])):
        turned = jnp.where(line == lane, value[:, 0:1], 0.0) + jnp.where(line + 16 == lane, value[:, 4:5], 0.0)
        best[k : k + 1, :] = jnp.sum(turned, axis=0, keepdims=True)[:, :GROUPS]


def vmem(count):
    return [pl.BlockSpec(memory_space=pltpu.VMEM)] * count


def ring_moved(piece, step):
    return lax.ppermute(piece, "zh", [(i, (i + step) % RING) for i in range(RING)])


def pack_kernel(w_query, w_key, w_value, w_out, packed):
    part = w_query.shape[0]
    half = part // 2
    packed[:part, :HD] = w_query[...]
    packed[:part, HD:] = w_key[...]
    packed[part : part + half, :HD] = w_value[:half, :]
    packed[part : part + half, HD:] = w_value[half:, :]
    packed[part + half :, :] = w_out[...]


def marks_of(owner, local, parity):
    at = lax.iota(jnp.int32, PAIRS)
    rank = jnp.max(
        jnp.where((owner[:, None] == owner[None, :]) & (at[:, None] > at[None, :]), 1, 0), axis=1
    )
    column = ((owner >> 5) << 1) | (owner & 1)
    code = ((owner >> 1) & 1) * 128 + column * SLOTS + ((owner >> 2) & 7) * 2 + rank
    label = lax.iota(jnp.int32, 128) + parity * 128
    marks = jnp.sum(jnp.where(code[None, :] == label[:, None], local[None, :] + 1, 0), axis=1)
    return code, marks.astype(BF)


def per_device(keys, slab, neighbour_ids, group_acts, table, norm_gain, w_query, w_key, w_value, w_out):
    y = lax.axis_index("pb")
    zh = lax.axis_index("zh")
    zl = lax.axis_index("zl")
    flat = neighbour_ids.T.reshape(PAIRS)
    owner = lax.div(flat, ROWS)
    local = flat - owner * ROWS
    quarter = lax.dynamic_slice_in_dim(slab, y * SLAB_ROWS, SLAB_ROWS, 0).astype(BF)
    numbers = jnp.pad(jnp.stack([owner, local]).astype(BF), ((0, KEYPAD - SLAB_ROWS - 2), (0, KEY - PAIRS)))
    pair = jnp.concatenate([quarter, numbers], axis=0)
    pair = lax.ppermute(pair, "zl", [(0, 1), (1, 0)])
    token = lax.dynamic_index_in_dim(table, y, axis=1, keepdims=False)
    both = jnp.concatenate([quarter, pair[:SLAB_ROWS]], axis=1)
    both = jnp.pad(both, ((0, 0), (0, E - 2 * KEY)))
    piece = jnp.concatenate([token, both], axis=0)
    right = [piece]
    left = [piece]
    for _ in range(3):
        right.append(ring_moved(right[-1], 1))
        left.append(ring_moved(left[-1], -1))
    far_a = ring_moved(right[3][:CUT], 1)
    far_b = ring_moved(left[3][CUT:], -1)
    pieces = [*right, left[3], left[2], left[1], far_a, far_b]
    packed = pl.pallas_call(
        pack_kernel,
        out_shape=jax.ShapeDtypeStruct((2 * w_query.shape[0], E), BF),
        in_specs=vmem(4),
        out_specs=pl.BlockSpec(memory_space=pltpu.VMEM),
    )(w_query, w_key, w_value, w_out)
    whole = lax.all_gather(packed, "pb", axis=0, tiled=False)
    part = w_query.shape[0]
    w_k = whole[:, :part, HD:].reshape(E, HD)
    w_v = whole[:, part : part + part // 2]
    w_v = jnp.concatenate([w_v[:, :, :HD], w_v[:, :, HD:]], axis=1).reshape(E, HD)
    acts = group_acts.reshape(GROUPS * CT, E)
    keyed = jnp.dot(acts, w_k, preferred_element_type=F32).astype(BF)
    valued = jnp.dot(acts, w_v, preferred_element_type=F32).astype(BF)
    tick = right[1][:8, :128]
    owner, local, pair, keys, tick = lax.optimization_barrier((owner, local, pair, keys, tick))
    code, own = marks_of(owner, local, zl)
    partner = pair[SLAB_ROWS : SLAB_ROWS + 2, :PAIRS].astype(jnp.int32)
    _, other = marks_of(partner[0], partner[1], zl)
    place = (code >> 7) * (PLANE * SLOTS) + (code & 127)
    place = place.reshape(2, GROUPS).T.reshape(GROUPS, 2, 1) + lax.iota(jnp.int32, NT) * 128
    place = place.reshape(PAIRS * NT, 1)
    sent = jnp.pad(keys.astype(BF), ((0, KEYPAD - GROUPS), (0, 0)))
    asks = jnp.stack([own.reshape(8, SLOTS), other.reshape(8, SLOTS)], axis=1)
    asks = jnp.pad(asks, ((0, 0), (GROUPS, KEYPAD - GROUPS - 2), (0, KEY - SLOTS)))
    sent = sent[None] + asks
    sent = jnp.broadcast_to(sent[None], (4, 8, KEYPAD, KEY)).reshape(PLANE, KEYPAD, KEY)
    asked = lax.all_to_all(sent, FLAT, split_axis=0, concat_axis=0, tiled=True)
    wanted = asked[:, GROUPS : GROUPS + 2, :SLOTS].astype(jnp.int32)
    wanted = jnp.where(zl == 0, jnp.stack([wanted[:, 0], wanted[:, 1]]), jnp.stack([wanted[:, 1], wanted[:, 0]]))
    away = jnp.bitwise_and(zh - lax.iota(jnp.int32, SLOTS) // 2 + RING, RING - 1)
    wanted = jnp.where(wanted > 0, away * ROWS + wanted - 1, -1).reshape(SERVERS * SLOTS, 1)
    wanted, keyed, valued = lax.optimization_barrier((wanted, keyed, valued))
    parity = jnp.full((1, 1, 128), zl, jnp.int32)
    served = pl.pallas_call(
        serve_kernel,
        out_shape=jax.ShapeDtypeStruct((SERVERS, SLOTS, WIDE), BF),
        in_specs=vmem(4 + RING + 1),
        out_specs=pl.BlockSpec(memory_space=pltpu.HBM),
        scratch_shapes=[
            pltpu.VMEM((RING * ROWS, E), BF),
            pltpu.VMEM((RING * 2 * SLAB_ROWS, KEY), F32),
            pltpu.VMEM((SERVERS, SLOTS, WIDE), BF),
            pltpu.SemaphoreType.DMA((4,)),
        ],
        compiler_params=pltpu.CompilerParams(vmem_limit_bytes=SERVE_LIMIT),
    )(parity, tick, wanted, asked, *pieces)
    got = lax.all_to_all(served, NEAR, split_axis=0, concat_axis=0, tiled=True)
    best, encoded = pl.pallas_call(
        layer_kernel,
        out_shape=(
            jax.ShapeDtypeStruct((2, GROUPS), F32),
            jax.ShapeDtypeStruct((GROUPS, 2, NT, E), BF),
        ),
        in_specs=[*vmem(4), pl.BlockSpec(memory_space=pltpu.HBM), *vmem(1)],
        out_specs=tuple(vmem(2)),
        scratch_shapes=[
            pltpu.VMEM((E, 2 * HD), BF),
            pltpu.VMEM((HD, E), BF),
            pltpu.SemaphoreType.DMA((8,)),
        ],
        compiler_params=pltpu.CompilerParams(vmem_limit_bytes=LIMIT),
    )(place, got, keyed, valued, whole, norm_gain.reshape(1, E))
    return best.T, encoded


def solution(mesh):
    split = Mesh(mesh.devices.reshape(4, RING, 2, 2, 4), SPLIT)
    return jax.shard_map(
        per_device,
        mesh=split,
        in_specs=(
            P(SPLIT, None),
            P(DB, None),
            P(SPLIT, None),
            P(SPLIT, None, None),
            P(DB, None, None),
            P(),
            P("pb", None),
            P("pb", None),
            P("pb", None),
            P("pb", None),
        ),
        out_specs=(P(SPLIT, None), P(SPLIT, None, None, None)),
        check_vma=False,
    )
```

```python
import jax
import jax.numpy as jnp
from jax import lax
from jax.experimental import pallas as pl
from jax.experimental.pallas import tpu as pltpu
from jax.sharding import Mesh
from jax.sharding import PartitionSpec as P

KEY = 384
E = 896
HEADS = 7
HSIZE = 64
HD = HEADS * HSIZE
NT = 4
CT = 4
ROWS = 96
GROUPS = 26
PAIRS = 2 * GROUPS
RING = 8
SLAB_ROWS = 24
PIECE = ROWS + SLAB_ROWS
PLANE = 32
SERVERS = 2 * PLANE
SLOTS = 16
KEYPAD = 32
WIDE = E + 128
LIMIT = 24 * 2**20
SERVE_LIMIT = 52 * 2**20
LOW = -1.0e38
SPLIT = ("x", "zh", "zl", "core", "pb")
DB = ("x", "zh", "zl", "core")
FLAT = ("pb", "x", "core")
NEAR = ("zl", *FLAT)
BF = jnp.bfloat16
F32 = jnp.float32


def best_two(hi, lo):
    count = hi.shape[0]
    while count > 1:
        half = count // 2
        h1, h2, l1, l2 = hi[:half], hi[half:count], lo[:half], lo[half:count]
        hi, lo = jnp.maximum(h1, h2), jnp.maximum(jnp.minimum(h1, h2), jnp.maximum(l1, l2))
        count = half
    return hi, lo


def serve_kernel(parity, code, keys, *refs):
    *pieces, sent, held, slab, out, sems = refs
    for k, piece in enumerate(pieces):
        held[k * ROWS : (k + 1) * ROWS, :] = piece[:ROWS, :]
        extra = piece[ROWS:, :]
        for part in range(2):
            at = (2 * k + part) * SLAB_ROWS
            slab[at : at + SLAB_ROWS, :] = extra[:, part * KEY : (part + 1) * KEY].astype(F32)
    wide = 512
    n = wide // KEYPAD
    rows = slab[...].astype(BF)
    mine = parity[...]
    for i in range(PLANE * KEYPAD // wide):
        block = keys[i * n : (i + 1) * n].reshape(wide, KEY)
        rating = lax.dot_general(
            rows, block, (((1,), (1,)), ((), ())), preferred_element_type=F32
        ) * (KEY**-0.5)
        h1, h2, h3 = rating[:128], rating[128:256], rating[256:]
        hi, lo = jnp.maximum(h1, h2), jnp.minimum(h1, h2)
        hi, lo = jnp.maximum(hi, h3), jnp.maximum(lo, jnp.minimum(hi, h3))
        hi, lo = best_two(hi, lo)
        hi_a = hi.astype(BF).astype(F32)
        lo_a = lo.astype(BF).astype(F32)
        line = lax.broadcasted_iota(jnp.int32, (16, wide), 0)
        parts = jnp.where(
            line == 0,
            hi_a,
            jnp.where(line == 1, hi - hi_a, jnp.where(line == 2, lo_a, jnp.where(line == 3, lo - lo_a, 0.0))),
        ).astype(BF)
        for half in range(2):
            unit = (
                lax.broadcasted_iota(jnp.int32, (16, 128), 0) + 4 * half
                == lax.broadcasted_iota(jnp.int32, (16, 128), 1)
            ).astype(F32).astype(BF)
            turned = lax.dot_general(
                parts, unit, (((0,), (0,)), ((), ())), preferred_element_type=F32
            ).reshape(n, 2, 16, 128)
            if half == 0:
                total = turned[:, 0]
            else:
                total = total + turned[:, 1]
        lane = lax.broadcasted_iota(jnp.int32, (1, 1, 128), 2)
        none = jnp.where(lax.rem(lane, 2) == 0, LOW, 0.0)
        for z in range(2):
            at = z * PLANE + i * n
            out[at : at + n, :, E:] = jnp.where(mine == z, total, none).astype(BF)
    step = 256
    n = step // SLOTS
    copies = []
    for i in range(SERVERS * SLOTS // step):
        label = lax.broadcasted_iota(jnp.int32, (step, RING * ROWS), 1)
        pick = (code[i * step : (i + 1) * step, :] == label).astype(F32).astype(BF)
        found = jnp.dot(pick, held[...], preferred_element_type=F32).astype(BF)
        out[i * n : (i + 1) * n, :, :E] = found.reshape(n, SLOTS, E)
        block = pl.ds(i * n, n)
        copies.append(pltpu.make_async_copy(out.at[block], sent.at[block], sems.at[i]))
        copies[-1].start()
    for copy in copies:
        copy.wait()


def layer_kernel(place, got, keyed, valued, w_query, w_out, gain, best, encoded):
    label = lax.broadcasted_iota(jnp.int32, (PAIRS * NT, SERVERS * SLOTS), 1)
    pick = (place[...] == label).astype(F32).astype(BF)
    rows = got[:, :, :E].reshape(SERVERS * SLOTS, E)
    x = jnp.dot(pick, rows, preferred_element_type=F32)
    square = jnp.mean(x * x, axis=-1, keepdims=True)
    normed = (x * lax.rsqrt(square + 1e-06) * gain[...]).astype(BF)
    query = jnp.dot(normed, w_query[...], preferred_element_type=F32).astype(BF)
    query = query.astype(F32)
    k_all = keyed[...]
    v_all = valued[...].astype(F32)
    head = lax.broadcasted_iota(jnp.int32, (1, HD), 1) // HSIZE
    mine = (
        lax.broadcasted_iota(jnp.int32, (PAIRS * NT, GROUPS * CT), 0) // (2 * NT)
        == lax.broadcasted_iota(jnp.int32, (PAIRS * NT, GROUPS * CT), 1) // CT
    )
    mixed = jnp.zeros((PAIRS * NT, HD), F32)
    for h in range(HEADS):
        q_h = jnp.where(head == h, query, 0.0).astype(BF)
        v_h = jnp.where(head == h, v_all, 0.0).astype(BF)
        logits = lax.dot_general(
            q_h, k_all, (((1,), (1,)), ((), ())), preferred_element_type=F32
        ) * (HSIZE**-0.5)
        logits = jnp.where(mine, logits, LOW)
        top = jnp.max(logits, axis=-1, keepdims=True)
        e = jnp.exp(logits - top)
        probs = (e / jnp.sum(e, axis=-1, keepdims=True)).astype(BF)
        mixed = mixed + jnp.dot(probs, v_h, preferred_element_type=F32)
    result = x + jnp.dot(mixed.astype(BF), w_out[...], preferred_element_type=F32)
    encoded[...] = result.astype(BF).reshape(GROUPS, 2, NT, E)
    c = got[:, :, E:].astype(F32)
    c = c + pltpu.roll(c, 127, 2)
    hi, lo = best_two(c, pltpu.roll(c, 126, 2))
    line = lax.broadcasted_iota(jnp.int32, (16, 128), 0)
    lane = lax.broadcasted_iota(jnp.int32, (16, 128), 1)
    for k, value in enumerate((hi[0], lo[0])):
        turned = jnp.where(line == lane, value[:, 0:1], 0.0) + jnp.where(line + 16 == lane, value[:, 4:5], 0.0)
        best[k : k + 1, :] = jnp.sum(turned, axis=0, keepdims=True)[:, :GROUPS]


def vmem(count):
    return [pl.BlockSpec(memory_space=pltpu.VMEM)] * count


def ring_moved(piece):
    pairs = []
    for at in range(RING):
        pairs.append((2 * at, 2 * ((at + 1) % RING)))
        pairs.append((2 * at + 1, 2 * ((at - 1) % RING) + 1))
    return lax.ppermute(piece, ("zh", "core"), pairs)


def pack_kernel(w_query, w_key, w_value, w_out, packed):
    part = w_query.shape[0]
    half = part // 2
    packed[:part, :HD] = w_query[...]
    packed[:part, HD:] = w_key[...]
    packed[part : part + half, :HD] = w_value[:half, :]
    packed[part : part + half, HD:] = w_value[half:, :]
    packed[part + half :, :] = w_out[...]


def project_kernel(acts, whole, keyed, valued, w_query, w_out, w_key, w_value):
    part = E // 4
    half = part // 2
    for b in range(4):
        at = b * part
        w_query[at : at + part, :] = whole[b, :part, :HD]
        w_key[at : at + part, :] = whole[b, :part, HD:]
        w_value[at : at + half, :] = whole[b, part : part + half, :HD]
        w_value[at + half : at + part, :] = whole[b, part : part + half, HD:]
        w_out[b * half : (b + 1) * half, :] = whole[b, part + half :, :]
    x = acts[...]
    keyed[...] = jnp.dot(x, w_key[...], preferred_element_type=F32).astype(BF)
    valued[...] = jnp.dot(x, w_value[...], preferred_element_type=F32).astype(BF)


def marks_of(owner, local, zh, parity):
    at = lax.iota(jnp.int32, PAIRS)
    rank = jnp.max(
        jnp.where((owner[:, None] == owner[None, :]) & (at[:, None] > at[None, :]), 1, 0), axis=1
    )
    core = owner & 1
    away = (zh - (owner >> 2)) & 7
    direct = (away & 3) == 0
    server = jnp.where(direct, core, away >> 2)
    steps = jnp.where(away > 4, 8 - away, away)
    slot = jnp.where(direct, 12 + (away >> 1), (steps - 1) * 4 + (core ^ server) * 2) + rank
    code = ((owner >> 1) & 1) * 128 + (((owner >> 5) << 1) | server) * SLOTS + slot
    label = lax.iota(jnp.int32, 128) + parity * 128
    marks = jnp.sum(jnp.where(code[None, :] == label[:, None], local[None, :] + 1, 0), axis=1)
    return code, marks.astype(BF)


def per_device(keys, slab, neighbour_ids, group_acts, table, norm_gain, w_query, w_key, w_value, w_out):
    y = lax.axis_index("pb")
    zh = lax.axis_index("zh")
    zl = lax.axis_index("zl")
    flat = neighbour_ids.T.reshape(PAIRS)
    owner = lax.div(flat, ROWS)
    local = flat - owner * ROWS
    quarter = lax.dynamic_slice_in_dim(slab, y * SLAB_ROWS, SLAB_ROWS, 0).astype(BF)
    numbers = jnp.pad(jnp.stack([owner, local]).astype(BF), ((0, KEYPAD - SLAB_ROWS - 2), (0, KEY - PAIRS)))
    pair = jnp.concatenate([quarter, numbers], axis=0)
    pair = lax.ppermute(pair, "zl", [(0, 1), (1, 0)])
    token = lax.dynamic_index_in_dim(table, y, axis=1, keepdims=False)
    both = jnp.concatenate([quarter, pair[:SLAB_ROWS]], axis=1)
    both = jnp.pad(both, ((0, 0), (0, E - 2 * KEY)))
    piece = jnp.concatenate([token, both], axis=0)
    ours = [piece]
    others = [lax.ppermute(piece, "core", [(0, 1), (1, 0)])]
    for _ in range(3):
        ours.append(ring_moved(ours[-1]))
        others.append(ring_moved(others[-1]))
    far = ring_moved(ours[3])
    pieces = [ours[1], others[1], ours[2], others[2], ours[3], others[3], ours[0], far]
    packed = pl.pallas_call(
        pack_kernel,
        out_shape=jax.ShapeDtypeStruct((2 * w_query.shape[0], E), BF),
        in_specs=vmem(4),
        out_specs=pl.BlockSpec(memory_space=pltpu.VMEM),
    )(w_query, w_key, w_value, w_out)
    whole = lax.all_gather(packed, "pb", axis=0, tiled=False)
    code, own = marks_of(owner, local, zh, zl)
    partner = pair[SLAB_ROWS : SLAB_ROWS + 2, :PAIRS].astype(jnp.int32)
    _, other = marks_of(partner[0], partner[1], zh, zl)
    place = (code >> 7) * (PLANE * SLOTS) + (code & 127)
    place = place.reshape(2, GROUPS).T.reshape(GROUPS, 2, 1) + lax.iota(jnp.int32, NT) * 128
    place = place.reshape(PAIRS * NT, 1)
    sent = jnp.pad(keys.astype(BF), ((0, KEYPAD - GROUPS), (0, 0)))
    asks = jnp.stack([own.reshape(8, SLOTS), other.reshape(8, SLOTS)], axis=1)
    asks = jnp.pad(asks, ((0, 0), (GROUPS, KEYPAD - GROUPS - 2), (0, KEY - SLOTS)))
    sent = sent[None] + asks
    sent = jnp.broadcast_to(sent[None], (4, 8, KEYPAD, KEY)).reshape(PLANE, KEYPAD, KEY)
    asked = lax.all_to_all(sent, FLAT, split_axis=0, concat_axis=0, tiled=True)
    wanted = asked[:, GROUPS : GROUPS + 2, :SLOTS].astype(jnp.int32)
    wanted = jnp.where(zl == 0, jnp.stack([wanted[:, 0], wanted[:, 1]]), jnp.stack([wanted[:, 1], wanted[:, 0]]))
    block = lax.iota(jnp.int32, SLOTS) // 2
    wanted = jnp.where(wanted > 0, block * ROWS + wanted - 1, -1).reshape(SERVERS * SLOTS, 1)
    parity = jnp.full((1, 1, 128), zl, jnp.int32)
    served = pl.pallas_call(
        serve_kernel,
        out_shape=jax.ShapeDtypeStruct((SERVERS, SLOTS, WIDE), BF),
        in_specs=vmem(3 + RING),
        out_specs=pl.BlockSpec(memory_space=pltpu.HBM),
        scratch_shapes=[
            pltpu.VMEM((RING * ROWS, E), BF),
            pltpu.VMEM((RING * 2 * SLAB_ROWS, KEY), F32),
            pltpu.VMEM((SERVERS, SLOTS, WIDE), BF),
            pltpu.SemaphoreType.DMA((4,)),
        ],
        compiler_params=pltpu.CompilerParams(vmem_limit_bytes=SERVE_LIMIT),
    )(parity, wanted, asked, *pieces)
    served, whole = lax.optimization_barrier((served, whole))
    got = lax.all_to_all(served, NEAR, split_axis=0, concat_axis=0, tiled=True)
    keyed, valued, w_q, w_o = pl.pallas_call(
        project_kernel,
        out_shape=(
            jax.ShapeDtypeStruct((GROUPS * CT, HD), BF),
            jax.ShapeDtypeStruct((GROUPS * CT, HD), BF),
            jax.ShapeDtypeStruct((E, HD), BF),
            jax.ShapeDtypeStruct((HD, E), BF),
        ),
        in_specs=vmem(2),
        out_specs=tuple(vmem(4)),
        scratch_shapes=[pltpu.VMEM((E, HD), BF), pltpu.VMEM((E, HD), BF)],
        compiler_params=pltpu.CompilerParams(vmem_limit_bytes=LIMIT),
    )(group_acts.reshape(GROUPS * CT, E), whole)
    best, encoded = pl.pallas_call(
        layer_kernel,
        out_shape=(
            jax.ShapeDtypeStruct((2, GROUPS), F32),
            jax.ShapeDtypeStruct((GROUPS, 2, NT, E), BF),
        ),
        in_specs=vmem(7),
        out_specs=tuple(vmem(2)),
        compiler_params=pltpu.CompilerParams(vmem_limit_bytes=LIMIT),
    )(place, got, keyed, valued, w_q, w_o, norm_gain.reshape(1, E))
    return best.T, encoded


def solution(mesh):
    split = Mesh(mesh.devices.reshape(4, RING, 2, 2, 4), SPLIT)
    return jax.shard_map(
        per_device,
        mesh=split,
        in_specs=(
            P(SPLIT, None),
            P(DB, None),
            P(SPLIT, None),
            P(SPLIT, None, None),
            P(DB, None, None),
            P(),
            P("pb", None),
            P("pb", None),
            P("pb", None),
            P("pb", None),
        ),
        out_specs=(P(SPLIT, None), P(SPLIT, None, None, None)),
        check_vma=False,
    )
```

```python
import jax
import jax.numpy as jnp
from jax import lax
from jax.experimental import pallas as pl
from jax.experimental.pallas import tpu as pltpu
from jax.sharding import Mesh
from jax.sharding import PartitionSpec as P

KEY = 384
E = 896
HEADS = 7
HSIZE = 64
HD = HEADS * HSIZE
NT = 4
CT = 4
ROWS = 96
GROUPS = 26
PAIRS = 2 * GROUPS
RING = 8
SLAB_ROWS = 24
PIECE = ROWS + SLAB_ROWS
PLANE = 32
SERVERS = 2 * PLANE
SLOTS = 16
KEYPAD = 32
WIDE = E + 128
LIMIT = 24 * 2**20
LAYER_LIMIT = 50 * 2**20
SERVE_LIMIT = 52 * 2**20
LOW = -1.0e38
SPLIT = ("x", "zh", "zl", "core", "pb")
DB = ("x", "zh", "zl", "core")
FLAT = ("pb", "x", "core")
NEAR = ("zl", *FLAT)
BF = jnp.bfloat16
F32 = jnp.float32


def best_two(hi, lo):
    count = hi.shape[0]
    while count > 1:
        half = count // 2
        h1, h2, l1, l2 = hi[:half], hi[half:count], lo[:half], lo[half:count]
        hi, lo = jnp.maximum(h1, h2), jnp.maximum(jnp.minimum(h1, h2), jnp.maximum(l1, l2))
        count = half
    return hi, lo


def serve_kernel(parity, code, keys, *refs):
    *pieces, sent, held, slab, out, sems = refs
    for k, piece in enumerate(pieces):
        held[k * ROWS : (k + 1) * ROWS, :] = piece[:ROWS, :]
        extra = piece[ROWS:, :]
        for part in range(2):
            at = (2 * k + part) * SLAB_ROWS
            slab[at : at + SLAB_ROWS, :] = extra[:, part * KEY : (part + 1) * KEY].astype(F32)
    wide = 512
    n = wide // KEYPAD
    rows = slab[...].astype(BF)
    mine = parity[...]
    for i in range(PLANE * KEYPAD // wide):
        block = keys[i * n : (i + 1) * n].reshape(wide, KEY)
        rating = lax.dot_general(
            rows, block, (((1,), (1,)), ((), ())), preferred_element_type=F32
        ) * (KEY**-0.5)
        h1, h2, h3 = rating[:128], rating[128:256], rating[256:]
        hi, lo = jnp.maximum(h1, h2), jnp.minimum(h1, h2)
        hi, lo = jnp.maximum(hi, h3), jnp.maximum(lo, jnp.minimum(hi, h3))
        hi, lo = best_two(hi, lo)
        hi_a = hi.astype(BF).astype(F32)
        lo_a = lo.astype(BF).astype(F32)
        line = lax.broadcasted_iota(jnp.int32, (16, wide), 0)
        parts = jnp.where(
            line == 0,
            hi_a,
            jnp.where(line == 1, hi - hi_a, jnp.where(line == 2, lo_a, jnp.where(line == 3, lo - lo_a, 0.0))),
        ).astype(BF)
        for half in range(2):
            unit = (
                lax.broadcasted_iota(jnp.int32, (16, 128), 0) + 4 * half
                == lax.broadcasted_iota(jnp.int32, (16, 128), 1)
            ).astype(F32).astype(BF)
            turned = lax.dot_general(
                parts, unit, (((0,), (0,)), ((), ())), preferred_element_type=F32
            ).reshape(n, 2, 16, 128)
            if half == 0:
                total = turned[:, 0]
            else:
                total = total + turned[:, 1]
        lane = lax.broadcasted_iota(jnp.int32, (1, 1, 128), 2)
        none = jnp.where(lax.rem(lane, 2) == 0, LOW, 0.0)
        for z in range(2):
            at = z * PLANE + i * n
            out[at : at + n, :, E:] = jnp.where(mine == z, total, none).astype(BF)
    step = 256
    n = step // SLOTS
    copies = []
    for i in range(SERVERS * SLOTS // step):
        label = lax.broadcasted_iota(jnp.int32, (step, RING * ROWS), 1)
        pick = (code[i * step : (i + 1) * step, :] == label).astype(F32).astype(BF)
        found = jnp.dot(pick, held[...], preferred_element_type=F32).astype(BF)
        out[i * n : (i + 1) * n, :, :E] = found.reshape(n, SLOTS, E)
        block = pl.ds(i * n, n)
        copies.append(pltpu.make_async_copy(out.at[block], sent.at[block], sems.at[i]))
        copies[-1].start()
    for copy in copies:
        copy.wait()


def layer_kernel(place, got, keyed, valued, w_query, w_out, gain, best, encoded):
    label = lax.broadcasted_iota(jnp.int32, (PAIRS * NT, SERVERS * SLOTS), 1)
    pick = (place[...] == label).astype(F32).astype(BF)
    rows = got[:, :, :E].reshape(SERVERS * SLOTS, E)
    x = jnp.dot(pick, rows, preferred_element_type=F32)
    square = jnp.mean(x * x, axis=-1, keepdims=True)
    normed = (x * lax.rsqrt(square + 1e-06) * gain[...]).astype(BF)
    query = jnp.dot(normed, w_query[...], preferred_element_type=F32).astype(BF)
    query = query.astype(F32)
    k_all = keyed[...]
    v_all = valued[...].astype(F32)
    head = lax.broadcasted_iota(jnp.int32, (1, HD), 1) // HSIZE
    mine = (
        lax.broadcasted_iota(jnp.int32, (PAIRS * NT, GROUPS * CT), 0) // (2 * NT)
        == lax.broadcasted_iota(jnp.int32, (PAIRS * NT, GROUPS * CT), 1) // CT
    )
    mixed = jnp.zeros((PAIRS * NT, HD), F32)
    for h in range(HEADS):
        q_h = jnp.where(head == h, query, 0.0).astype(BF)
        v_h = jnp.where(head == h, v_all, 0.0).astype(BF)
        logits = lax.dot_general(
            q_h, k_all, (((1,), (1,)), ((), ())), preferred_element_type=F32
        ) * (HSIZE**-0.5)
        logits = jnp.where(mine, logits, LOW)
        top = jnp.max(logits, axis=-1, keepdims=True)
        e = jnp.exp(logits - top)
        probs = (e / jnp.sum(e, axis=-1, keepdims=True)).astype(BF)
        mixed = mixed + jnp.dot(probs, v_h, preferred_element_type=F32)
    result = x + jnp.dot(mixed.astype(BF), w_out[...], preferred_element_type=F32)
    encoded[...] = result.astype(BF).reshape(GROUPS, 2, NT, E)
    c = got[:, :, E:].astype(F32)
    c = c + pltpu.roll(c, 127, 2)
    hi, lo = best_two(c, pltpu.roll(c, 126, 2))
    line = lax.broadcasted_iota(jnp.int32, (16, 128), 0)
    lane = lax.broadcasted_iota(jnp.int32, (16, 128), 1)
    for k, value in enumerate((hi[0], lo[0])):
        turned = jnp.where(line == lane, value[:, 0:1], 0.0) + jnp.where(line + 16 == lane, value[:, 4:5], 0.0)
        best[k : k + 1, :] = jnp.sum(turned, axis=0, keepdims=True)[:, :GROUPS]


def vmem(count):
    return [pl.BlockSpec(memory_space=pltpu.VMEM)] * count


def ring_moved(piece):
    pairs = []
    for at in range(RING):
        pairs.append((2 * at, 2 * ((at + 1) % RING)))
        pairs.append((2 * at + 1, 2 * ((at - 1) % RING) + 1))
    return lax.ppermute(piece, ("zh", "core"), pairs)


def pack_kernel(w_query, w_key, w_value, w_out, packed):
    part = w_query.shape[0]
    half = part // 2
    packed[:part, :HD] = w_query[...]
    packed[:part, HD:] = w_key[...]
    packed[part : part + half, :HD] = w_value[:half, :]
    packed[part : part + half, HD:] = w_value[half:, :]
    packed[part + half :, :] = w_out[...]


def project_kernel(acts, whole, keyed, valued, w_query, w_out, w_key, w_value):
    part = E // 4
    half = part // 2
    for b in range(4):
        at = b * part
        w_query[at : at + part, :] = whole[b, :part, :HD]
        w_key[at : at + part, :] = whole[b, :part, HD:]
        w_value[at : at + half, :] = whole[b, part : part + half, :HD]
        w_value[at + half : at + part, :] = whole[b, part : part + half, HD:]
        w_out[b * half : (b + 1) * half, :] = whole[b, part + half :, :]
    x = acts[...]
    keyed[...] = jnp.dot(x, w_key[...], preferred_element_type=F32).astype(BF)
    valued[...] = jnp.dot(x, w_value[...], preferred_element_type=F32).astype(BF)


def marks_of(owner, local, zh, parity):
    at = lax.iota(jnp.int32, PAIRS)
    rank = jnp.max(
        jnp.where((owner[:, None] == owner[None, :]) & (at[:, None] > at[None, :]), 1, 0), axis=1
    )
    core = owner & 1
    away = (zh - (owner >> 2)) & 7
    direct = (away & 3) == 0
    server = jnp.where(direct, core, away >> 2)
    steps = jnp.where(away > 4, 8 - away, away)
    slot = jnp.where(direct, 12 + (away >> 1), (steps - 1) * 4 + (core ^ server) * 2) + rank
    code = ((owner >> 1) & 1) * 128 + (((owner >> 5) << 1) | server) * SLOTS + slot
    label = lax.iota(jnp.int32, 128) + parity * 128
    marks = jnp.sum(jnp.where(code[None, :] == label[:, None], local[None, :] + 1, 0), axis=1)
    return code, marks.astype(BF)


def per_device(keys, slab, neighbour_ids, group_acts, table, norm_gain, w_query, w_key, w_value, w_out):
    y = lax.axis_index("pb")
    zh = lax.axis_index("zh")
    zl = lax.axis_index("zl")
    flat = neighbour_ids.T.reshape(PAIRS)
    owner = lax.div(flat, ROWS)
    local = flat - owner * ROWS
    quarter = lax.dynamic_slice_in_dim(slab, y * SLAB_ROWS, SLAB_ROWS, 0).astype(BF)
    numbers = jnp.pad(jnp.stack([owner, local]).astype(BF), ((0, KEYPAD - SLAB_ROWS - 2), (0, KEY - PAIRS)))
    pair = jnp.concatenate([quarter, numbers], axis=0)
    pair, w_query, w_key, w_value, w_out = lax.optimization_barrier((pair, w_query, w_key, w_value, w_out))
    pair = lax.ppermute(pair, "zl", [(0, 1), (1, 0)])
    packed = pl.pallas_call(
        pack_kernel,
        out_shape=jax.ShapeDtypeStruct((2 * w_query.shape[0], E), BF),
        in_specs=vmem(4),
        out_specs=pl.BlockSpec(memory_space=pltpu.VMEM),
    )(w_query, w_key, w_value, w_out)
    token = lax.dynamic_index_in_dim(table, y, axis=1, keepdims=False)
    both = jnp.concatenate([quarter, pair[:SLAB_ROWS]], axis=1)
    both = jnp.pad(both, ((0, 0), (0, E - 2 * KEY)))
    piece = jnp.concatenate([token, both], axis=0)
    ours = [piece]
    others = [lax.ppermute(piece, "core", [(0, 1), (1, 0)])]
    for _ in range(3):
        ours.append(ring_moved(ours[-1]))
        others.append(ring_moved(others[-1]))
    far = ring_moved(ours[3])
    pieces = [ours[1], others[1], ours[2], others[2], ours[3], others[3], ours[0], far]
    whole = lax.all_gather(packed, "pb", axis=0, tiled=False)
    code, own = marks_of(owner, local, zh, zl)
    partner = pair[SLAB_ROWS : SLAB_ROWS + 2, :PAIRS].astype(jnp.int32)
    _, other = marks_of(partner[0], partner[1], zh, zl)
    place = (code >> 7) * (PLANE * SLOTS) + (code & 127)
    place = place.reshape(2, GROUPS).T.reshape(GROUPS, 2, 1) + lax.iota(jnp.int32, NT) * 128
    place = place.reshape(PAIRS * NT, 1)
    sent = jnp.pad(keys.astype(BF), ((0, KEYPAD - GROUPS), (0, 0)))
    asks = jnp.stack([own.reshape(8, SLOTS), other.reshape(8, SLOTS)], axis=1)
    asks = jnp.pad(asks, ((0, 0), (GROUPS, KEYPAD - GROUPS - 2), (0, KEY - SLOTS)))
    sent = sent[None] + asks
    sent = jnp.broadcast_to(sent[None], (4, 8, KEYPAD, KEY)).reshape(PLANE, KEYPAD, KEY)
    asked = lax.all_to_all(sent, FLAT, split_axis=0, concat_axis=0, tiled=True)
    wanted = asked[:, GROUPS : GROUPS + 2, :SLOTS].astype(jnp.int32)
    wanted = jnp.where(zl == 0, jnp.stack([wanted[:, 0], wanted[:, 1]]), jnp.stack([wanted[:, 1], wanted[:, 0]]))
    block = lax.iota(jnp.int32, SLOTS) // 2
    wanted = jnp.where(wanted > 0, block * ROWS + wanted - 1, -1).reshape(SERVERS * SLOTS, 1)
    parity = jnp.full((1, 1, 128), zl, jnp.int32)
    served = pl.pallas_call(
        serve_kernel,
        out_shape=jax.ShapeDtypeStruct((SERVERS, SLOTS, WIDE), BF),
        in_specs=vmem(3 + RING),
        out_specs=pl.BlockSpec(memory_space=pltpu.HBM),
        scratch_shapes=[
            pltpu.VMEM((RING * ROWS, E), BF),
            pltpu.VMEM((RING * 2 * SLAB_ROWS, KEY), F32),
            pltpu.VMEM((SERVERS, SLOTS, WIDE), BF),
            pltpu.SemaphoreType.DMA((4,)),
        ],
        compiler_params=pltpu.CompilerParams(vmem_limit_bytes=SERVE_LIMIT),
    )(parity, wanted, asked, *pieces)
    served, whole = lax.optimization_barrier((served, whole))
    got = lax.all_to_all(served, NEAR, split_axis=0, concat_axis=0, tiled=True)
    keyed, valued, w_q, w_o = pl.pallas_call(
        project_kernel,
        out_shape=(
            jax.ShapeDtypeStruct((GROUPS * CT, HD), BF),
            jax.ShapeDtypeStruct((GROUPS * CT, HD), BF),
            jax.ShapeDtypeStruct((E, HD), BF),
            jax.ShapeDtypeStruct((HD, E), BF),
        ),
        in_specs=vmem(2),
        out_specs=tuple(vmem(4)),
        scratch_shapes=[pltpu.VMEM((E, HD), BF), pltpu.VMEM((E, HD), BF)],
        compiler_params=pltpu.CompilerParams(vmem_limit_bytes=LIMIT),
    )(group_acts.reshape(GROUPS * CT, E), whole)
    best, encoded = pl.pallas_call(
        layer_kernel,
        out_shape=(
            jax.ShapeDtypeStruct((2, GROUPS), F32),
            jax.ShapeDtypeStruct((GROUPS, 2, NT, E), BF),
        ),
        in_specs=vmem(7),
        out_specs=tuple(vmem(2)),
        compiler_params=pltpu.CompilerParams(vmem_limit_bytes=LAYER_LIMIT),
    )(place, got, keyed, valued, w_q, w_o, norm_gain.reshape(1, E))
    return best.T, encoded


def solution(mesh):
    split = Mesh(mesh.devices.reshape(4, RING, 2, 2, 4), SPLIT)
    return jax.shard_map(
        per_device,
        mesh=split,
        in_specs=(
            P(SPLIT, None),
            P(DB, None),
            P(SPLIT, None),
            P(SPLIT, None, None),
            P(DB, None, None),
            P(),
            P("pb", None),
            P("pb", None),
            P("pb", None),
            P("pb", None),
        ),
        out_specs=(P(SPLIT, None), P(SPLIT, None, None, None)),
        check_vma=False,
    )
```

```python
import jax
import jax.numpy as jnp
from jax import lax
from jax.experimental import pallas as pl
from jax.experimental.pallas import tpu as pltpu
from jax.sharding import Mesh
from jax.sharding import PartitionSpec as P

KEY = 384
E = 896
HEADS = 7
HSIZE = 64
HD = HEADS * HSIZE
NT = 4
CT = 4
ROWS = 96
GROUPS = 26
PAIRS = 2 * GROUPS
RING = 8
SLAB_ROWS = 24
PIECE = ROWS + SLAB_ROWS
PLANE = 32
SERVERS = 2 * PLANE
SLOTS = 16
KEYPAD = 32
WIDE = E + 128
LIMIT = 24 * 2**20
LAYER_LIMIT = 50 * 2**20
SERVE_LIMIT = 52 * 2**20
LOW = -1.0e38
SPLIT = ("x", "zh", "zl", "core", "pb")
DB = ("x", "zh", "zl", "core")
FLAT = ("pb", "x", "core")
NEAR = ("zl", *FLAT)
BF = jnp.bfloat16
F32 = jnp.float32


def best_two(hi, lo):
    count = hi.shape[0]
    while count > 1:
        half = count // 2
        h1, h2, l1, l2 = hi[:half], hi[half:count], lo[:half], lo[half:count]
        hi, lo = jnp.maximum(h1, h2), jnp.maximum(jnp.minimum(h1, h2), jnp.maximum(l1, l2))
        count = half
    return hi, lo


def serve_kernel(parity, code, keys, *refs):
    *pieces, sent, held, slab, out, sems = refs
    for k, piece in enumerate(pieces):
        held[k * ROWS : (k + 1) * ROWS, :] = piece[:ROWS, :]
        extra = piece[ROWS:, :]
        for part in range(2):
            at = (2 * k + part) * SLAB_ROWS
            slab[at : at + SLAB_ROWS, :] = extra[:, part * KEY : (part + 1) * KEY].astype(F32)
    wide = 512
    n = wide // KEYPAD
    rows = slab[...].astype(BF)
    mine = parity[...]
    for i in range(PLANE * KEYPAD // wide):
        block = keys[i * n : (i + 1) * n].reshape(wide, KEY)
        rating = lax.dot_general(
            rows, block, (((1,), (1,)), ((), ())), preferred_element_type=F32
        ) * (KEY**-0.5)
        h1, h2, h3 = rating[:128], rating[128:256], rating[256:]
        hi, lo = jnp.maximum(h1, h2), jnp.minimum(h1, h2)
        hi, lo = jnp.maximum(hi, h3), jnp.maximum(lo, jnp.minimum(hi, h3))
        hi, lo = best_two(hi, lo)
        hi_a = hi.astype(BF).astype(F32)
        lo_a = lo.astype(BF).astype(F32)
        line = lax.broadcasted_iota(jnp.int32, (16, wide), 0)
        parts = jnp.where(
            line == 0,
            hi_a,
            jnp.where(line == 1, hi - hi_a, jnp.where(line == 2, lo_a, jnp.where(line == 3, lo - lo_a, 0.0))),
        ).astype(BF)
        for half in range(2):
            unit = (
                lax.broadcasted_iota(jnp.int32, (16, 128), 0) + 4 * half
                == lax.broadcasted_iota(jnp.int32, (16, 128), 1)
            ).astype(F32).astype(BF)
            turned = lax.dot_general(
                parts, unit, (((0,), (0,)), ((), ())), preferred_element_type=F32
            ).reshape(n, 2, 16, 128)
            if half == 0:
                total = turned[:, 0]
            else:
                total = total + turned[:, 1]
        lane = lax.broadcasted_iota(jnp.int32, (1, 1, 128), 2)
        none = jnp.where(lax.rem(lane, 2) == 0, LOW, 0.0)
        for z in range(2):
            at = z * PLANE + i * n
            out[at : at + n, :, E:] = jnp.where(mine == z, total, none).astype(BF)
    step = 256
    n = step // SLOTS
    copies = []
    for i in range(SERVERS * SLOTS // step):
        label = lax.broadcasted_iota(jnp.int32, (step, RING * ROWS), 1)
        pick = (code[i * step : (i + 1) * step, :] == label).astype(F32).astype(BF)
        found = jnp.dot(pick, held[...], preferred_element_type=F32).astype(BF)
        out[i * n : (i + 1) * n, :, :E] = found.reshape(n, SLOTS, E)
        block = pl.ds(i * n, n)
        copies.append(pltpu.make_async_copy(out.at[block], sent.at[block], sems.at[i]))
        copies[-1].start()
    for copy in copies:
        copy.wait()


def layer_kernel(place, got, keyed, valued, w_query, w_out, gain, best, encoded):
    label = lax.broadcasted_iota(jnp.int32, (PAIRS * NT, SERVERS * SLOTS), 1)
    pick = (place[...] == label).astype(F32).astype(BF)
    rows = got[:, :, :E].reshape(SERVERS * SLOTS, E)
    x = jnp.dot(pick, rows, preferred_element_type=F32)
    square = jnp.mean(x * x, axis=-1, keepdims=True)
    normed = (x * lax.rsqrt(square + 1e-06) * gain[...]).astype(BF)
    query = jnp.dot(normed, w_query[...], preferred_element_type=F32).astype(BF)
    query = query.astype(F32)
    k_all = keyed[...]
    v_all = valued[...].astype(F32)
    head = lax.broadcasted_iota(jnp.int32, (1, HD), 1) // HSIZE
    mine = (
        lax.broadcasted_iota(jnp.int32, (PAIRS * NT, GROUPS * CT), 0) // (2 * NT)
        == lax.broadcasted_iota(jnp.int32, (PAIRS * NT, GROUPS * CT), 1) // CT
    )
    mixed = jnp.zeros((PAIRS * NT, HD), F32)
    for h in range(HEADS):
        q_h = jnp.where(head == h, query, 0.0).astype(BF)
        v_h = jnp.where(head == h, v_all, 0.0).astype(BF)
        logits = lax.dot_general(
            q_h, k_all, (((1,), (1,)), ((), ())), preferred_element_type=F32
        ) * (HSIZE**-0.5)
        logits = jnp.where(mine, logits, LOW)
        top = jnp.max(logits, axis=-1, keepdims=True)
        e = jnp.exp(logits - top)
        probs = (e / jnp.sum(e, axis=-1, keepdims=True)).astype(BF)
        mixed = mixed + jnp.dot(probs, v_h, preferred_element_type=F32)
    result = x + jnp.dot(mixed.astype(BF), w_out[...], preferred_element_type=F32)
    encoded[...] = result.astype(BF).reshape(GROUPS, 2, NT, E)
    c = got[:, :, E:].astype(F32)
    c = c + pltpu.roll(c, 127, 2)
    hi, lo = best_two(c, pltpu.roll(c, 126, 2))
    line = lax.broadcasted_iota(jnp.int32, (16, 128), 0)
    lane = lax.broadcasted_iota(jnp.int32, (16, 128), 1)
    for k, value in enumerate((hi[0], lo[0])):
        turned = jnp.where(line == lane, value[:, 0:1], 0.0) + jnp.where(line + 16 == lane, value[:, 4:5], 0.0)
        best[k : k + 1, :] = jnp.sum(turned, axis=0, keepdims=True)[:, :GROUPS]


def vmem(count):
    return [pl.BlockSpec(memory_space=pltpu.VMEM)] * count


def ring_moved(piece, crossed=0):
    pairs = []
    for at in range(RING):
        pairs.append((2 * at + crossed, 2 * ((at + 1) % RING)))
        pairs.append((2 * at + 1 - crossed, 2 * ((at - 1) % RING) + 1))
    return lax.ppermute(piece, ("zh", "core"), pairs)


def pack_kernel(w_query, w_key, w_value, w_out, packed):
    part = w_query.shape[0]
    half = part // 2
    packed[:part, :HD] = w_query[...]
    packed[:part, HD:] = w_key[...]
    packed[part : part + half, :HD] = w_value[:half, :]
    packed[part : part + half, HD:] = w_value[half:, :]
    packed[part + half :, :] = w_out[...]


def project_kernel(acts, whole, keyed, valued, w_query, w_out, w_key, w_value):
    part = E // 4
    half = part // 2
    for b in range(4):
        at = b * part
        w_query[at : at + part, :] = whole[b, :part, :HD]
        w_key[at : at + part, :] = whole[b, :part, HD:]
        w_value[at : at + half, :] = whole[b, part : part + half, :HD]
        w_value[at + half : at + part, :] = whole[b, part : part + half, HD:]
        w_out[b * half : (b + 1) * half, :] = whole[b, part + half :, :]
    x = acts[...]
    keyed[...] = jnp.dot(x, w_key[...], preferred_element_type=F32).astype(BF)
    valued[...] = jnp.dot(x, w_value[...], preferred_element_type=F32).astype(BF)


def marks_of(owner, local, zh, parity):
    at = lax.iota(jnp.int32, PAIRS)
    rank = jnp.max(
        jnp.where((owner[:, None] == owner[None, :]) & (at[:, None] > at[None, :]), 1, 0), axis=1
    )
    core = owner & 1
    away = (zh - (owner >> 2)) & 7
    direct = (away & 3) == 0
    server = jnp.where(direct, core, away >> 2)
    steps = jnp.where(away > 4, 8 - away, away)
    slot = jnp.where(direct, 12 + (away >> 1), (steps - 1) * 4 + (core ^ server) * 2) + rank
    code = ((owner >> 1) & 1) * 128 + (((owner >> 5) << 1) | server) * SLOTS + slot
    label = lax.iota(jnp.int32, 128) + parity * 128
    marks = jnp.sum(jnp.where(code[None, :] == label[:, None], local[None, :] + 1, 0), axis=1)
    return code, marks.astype(BF)


def per_device(keys, slab, neighbour_ids, group_acts, table, norm_gain, w_query, w_key, w_value, w_out):
    y = lax.axis_index("pb")
    zh = lax.axis_index("zh")
    zl = lax.axis_index("zl")
    flat = neighbour_ids.T.reshape(PAIRS)
    owner = lax.div(flat, ROWS)
    local = flat - owner * ROWS
    quarter = lax.dynamic_slice_in_dim(slab, y * SLAB_ROWS, SLAB_ROWS, 0).astype(BF)
    numbers = jnp.pad(jnp.stack([owner, local]).astype(BF), ((0, KEYPAD - SLAB_ROWS - 2), (0, KEY - PAIRS)))
    pair = jnp.concatenate([quarter, numbers], axis=0)
    pair, w_query, w_key, w_value, w_out = lax.optimization_barrier((pair, w_query, w_key, w_value, w_out))
    pair = lax.ppermute(pair, "zl", [(0, 1), (1, 0)])
    packed = pl.pallas_call(
        pack_kernel,
        out_shape=jax.ShapeDtypeStruct((2 * w_query.shape[0], E), BF),
        in_specs=vmem(4),
        out_specs=pl.BlockSpec(memory_space=pltpu.VMEM),
    )(w_query, w_key, w_value, w_out)
    token = lax.dynamic_index_in_dim(table, y, axis=1, keepdims=False)
    both = jnp.concatenate([quarter, pair[:SLAB_ROWS]], axis=1)
    both = jnp.pad(both, ((0, 0), (0, E - 2 * KEY)))
    piece = jnp.concatenate([token, both], axis=0)
    ours = [piece]
    others = [piece]
    for k in range(3):
        ours.append(ring_moved(ours[-1]))
        others.append(ring_moved(others[-1], crossed=1 if k == 0 else 0))
    far = ring_moved(ours[3])
    pieces = [ours[1], others[1], ours[2], others[2], ours[3], others[3], ours[0], far]
    whole = lax.all_gather(packed, "pb", axis=0, tiled=False)
    code, own = marks_of(owner, local, zh, zl)
    partner = pair[SLAB_ROWS : SLAB_ROWS + 2, :PAIRS].astype(jnp.int32)
    _, other = marks_of(partner[0], partner[1], zh, zl)
    place = (code >> 7) * (PLANE * SLOTS) + (code & 127)
    place = place.reshape(2, GROUPS).T.reshape(GROUPS, 2, 1) + lax.iota(jnp.int32, NT) * 128
    place = place.reshape(PAIRS * NT, 1)
    sent = jnp.pad(keys.astype(BF), ((0, KEYPAD - GROUPS), (0, 0)))
    asks = jnp.stack([own.reshape(8, SLOTS), other.reshape(8, SLOTS)], axis=1)
    asks = jnp.pad(asks, ((0, 0), (GROUPS, KEYPAD - GROUPS - 2), (0, KEY - SLOTS)))
    sent = sent[None] + asks
    sent = jnp.broadcast_to(sent[None], (4, 8, KEYPAD, KEY)).reshape(PLANE, KEYPAD, KEY)
    asked = lax.all_to_all(sent, FLAT, split_axis=0, concat_axis=0, tiled=True)
    wanted = asked[:, GROUPS : GROUPS + 2, :SLOTS].astype(jnp.int32)
    wanted = jnp.where(zl == 0, jnp.stack([wanted[:, 0], wanted[:, 1]]), jnp.stack([wanted[:, 1], wanted[:, 0]]))
    block = lax.iota(jnp.int32, SLOTS) // 2
    wanted = jnp.where(wanted > 0, block * ROWS + wanted - 1, -1).reshape(SERVERS * SLOTS, 1)
    parity = jnp.full((1, 1, 128), zl, jnp.int32)
    served = pl.pallas_call(
        serve_kernel,
        out_shape=jax.ShapeDtypeStruct((SERVERS, SLOTS, WIDE), BF),
        in_specs=vmem(3 + RING),
        out_specs=pl.BlockSpec(memory_space=pltpu.HBM),
        scratch_shapes=[
            pltpu.VMEM((RING * ROWS, E), BF),
            pltpu.VMEM((RING * 2 * SLAB_ROWS, KEY), F32),
            pltpu.VMEM((SERVERS, SLOTS, WIDE), BF),
            pltpu.SemaphoreType.DMA((4,)),
        ],
        compiler_params=pltpu.CompilerParams(vmem_limit_bytes=SERVE_LIMIT),
    )(parity, wanted, asked, *pieces)
    served, whole = lax.optimization_barrier((served, whole))
    got = lax.all_to_all(served, NEAR, split_axis=0, concat_axis=0, tiled=True)
    keyed, valued, w_q, w_o = pl.pallas_call(
        project_kernel,
        out_shape=(
            jax.ShapeDtypeStruct((GROUPS * CT, HD), BF),
            jax.ShapeDtypeStruct((GROUPS * CT, HD), BF),
            jax.ShapeDtypeStruct((E, HD), BF),
            jax.ShapeDtypeStruct((HD, E), BF),
        ),
        in_specs=vmem(2),
        out_specs=tuple(vmem(4)),
        scratch_shapes=[pltpu.VMEM((E, HD), BF), pltpu.VMEM((E, HD), BF)],
        compiler_params=pltpu.CompilerParams(vmem_limit_bytes=LIMIT),
    )(group_acts.reshape(GROUPS * CT, E), whole)
    best, encoded = pl.pallas_call(
        layer_kernel,
        out_shape=(
            jax.ShapeDtypeStruct((2, GROUPS), F32),
            jax.ShapeDtypeStruct((GROUPS, 2, NT, E), BF),
        ),
        in_specs=vmem(7),
        out_specs=tuple(vmem(2)),
        compiler_params=pltpu.CompilerParams(vmem_limit_bytes=LAYER_LIMIT),
    )(place, got, keyed, valued, w_q, w_o, norm_gain.reshape(1, E))
    return best.T, encoded


def solution(mesh):
    split = Mesh(mesh.devices.reshape(4, RING, 2, 2, 4), SPLIT)
    return jax.shard_map(
        per_device,
        mesh=split,
        in_specs=(
            P(SPLIT, None),
            P(DB, None),
            P(SPLIT, None),
            P(SPLIT, None, None),
            P(DB, None, None),
            P(),
            P("pb", None),
            P("pb", None),
            P("pb", None),
            P("pb", None),
        ),
        out_specs=(P(SPLIT, None), P(SPLIT, None, None, None)),
        check_vma=False,
    )
```

```python
import jax
import jax.numpy as jnp
from jax import lax
from jax.experimental import pallas as pl
from jax.experimental.pallas import tpu as pltpu
from jax.sharding import Mesh
from jax.sharding import PartitionSpec as P

KEY = 384
E = 896
HEADS = 7
HSIZE = 64
HD = HEADS * HSIZE
NT = 4
CT = 4
ROWS = 96
GROUPS = 26
PAIRS = 2 * GROUPS
RING = 8
SLAB_ROWS = 24
PIECE = ROWS + SLAB_ROWS
PLANE = 32
SERVERS = 2 * PLANE
SLOTS = 16
KEYPAD = 32
WIDE = E + 128
LIMIT = 24 * 2**20
LAYER_LIMIT = 50 * 2**20
SERVE_LIMIT = 52 * 2**20
LOW = -1.0e38
SPLIT = ("x", "zh", "zl", "core", "pb")
DB = ("x", "zh", "zl", "core")
FLAT = ("pb", "x", "core")
NEAR = ("zl", *FLAT)
BF = jnp.bfloat16
F32 = jnp.float32


def best_two(hi, lo):
    count = hi.shape[0]
    while count > 1:
        half = count // 2
        h1, h2, l1, l2 = hi[:half], hi[half:count], lo[:half], lo[half:count]
        hi, lo = jnp.maximum(h1, h2), jnp.maximum(jnp.minimum(h1, h2), jnp.maximum(l1, l2))
        count = half
    return hi, lo


def serve_kernel(parity, code, keys, *refs):
    *pieces, sent, held, slab, out, sems = refs
    for k, piece in enumerate(pieces):
        held[k * ROWS : (k + 1) * ROWS, :] = piece[:ROWS, :]
        extra = piece[ROWS:, :]
        for part in range(2):
            at = (2 * k + part) * SLAB_ROWS
            slab[at : at + SLAB_ROWS, :] = extra[:, part * KEY : (part + 1) * KEY].astype(F32)
    wide = 512
    n = wide // KEYPAD
    rows = slab[...].astype(BF)
    mine = parity[...]
    for i in range(PLANE * KEYPAD // wide):
        block = keys[i * n : (i + 1) * n].reshape(wide, KEY)
        rating = lax.dot_general(
            rows, block, (((1,), (1,)), ((), ())), preferred_element_type=F32
        ) * (KEY**-0.5)
        h1, h2, h3 = rating[:128], rating[128:256], rating[256:]
        hi, lo = jnp.maximum(h1, h2), jnp.minimum(h1, h2)
        hi, lo = jnp.maximum(hi, h3), jnp.maximum(lo, jnp.minimum(hi, h3))
        hi, lo = best_two(hi, lo)
        hi_a = hi.astype(BF).astype(F32)
        lo_a = lo.astype(BF).astype(F32)
        line = lax.broadcasted_iota(jnp.int32, (16, wide), 0)
        parts = jnp.where(
            line == 0,
            hi_a,
            jnp.where(line == 1, hi - hi_a, jnp.where(line == 2, lo_a, jnp.where(line == 3, lo - lo_a, 0.0))),
        ).astype(BF)
        for half in range(2):
            unit = (
                lax.broadcasted_iota(jnp.int32, (16, 128), 0) + 4 * half
                == lax.broadcasted_iota(jnp.int32, (16, 128), 1)
            ).astype(F32).astype(BF)
            turned = lax.dot_general(
                parts, unit, (((0,), (0,)), ((), ())), preferred_element_type=F32
            ).reshape(n, 2, 16, 128)
            if half == 0:
                total = turned[:, 0]
            else:
                total = total + turned[:, 1]
        lane = lax.broadcasted_iota(jnp.int32, (1, 1, 128), 2)
        none = jnp.where(lax.rem(lane, 2) == 0, LOW, 0.0)
        for z in range(2):
            at = z * PLANE + i * n
            out[at : at + n, :, E:] = jnp.where(mine == z, total, none).astype(BF)
    step = 256
    n = step // SLOTS
    copies = []
    for i in range(SERVERS * SLOTS // step):
        label = lax.broadcasted_iota(jnp.int32, (step, RING * ROWS), 1)
        pick = (code[i * step : (i + 1) * step, :] == label).astype(F32).astype(BF)
        found = jnp.dot(pick, held[...], preferred_element_type=F32).astype(BF)
        out[i * n : (i + 1) * n, :, :E] = found.reshape(n, SLOTS, E)
        block = pl.ds(i * n, n)
        copies.append(pltpu.make_async_copy(out.at[block], sent.at[block], sems.at[i]))
        copies[-1].start()
    for copy in copies:
        copy.wait()


def layer_kernel(place, got, keyed, valued, w_query, w_out, gain, best, encoded):
    label = lax.broadcasted_iota(jnp.int32, (PAIRS * NT, SERVERS * SLOTS), 1)
    pick = (place[...] == label).astype(F32).astype(BF)
    rows = got[:, :, :E].reshape(SERVERS * SLOTS, E)
    x = jnp.dot(pick, rows, preferred_element_type=F32)
    square = jnp.mean(x * x, axis=-1, keepdims=True)
    normed = (x * lax.rsqrt(square + 1e-06) * gain[...]).astype(BF)
    query = jnp.dot(normed, w_query[...], preferred_element_type=F32).astype(BF)
    query = query.astype(F32)
    k_all = keyed[...]
    v_all = valued[...].astype(F32)
    head = lax.broadcasted_iota(jnp.int32, (1, HD), 1) // HSIZE
    mine = (
        lax.broadcasted_iota(jnp.int32, (PAIRS * NT, GROUPS * CT), 0) // (2 * NT)
        == lax.broadcasted_iota(jnp.int32, (PAIRS * NT, GROUPS * CT), 1) // CT
    )
    mixed = jnp.zeros((PAIRS * NT, HD), F32)
    for h in range(HEADS):
        q_h = jnp.where(head == h, query, 0.0).astype(BF)
        v_h = jnp.where(head == h, v_all, 0.0).astype(BF)
        logits = lax.dot_general(
            q_h, k_all, (((1,), (1,)), ((), ())), preferred_element_type=F32
        ) * (HSIZE**-0.5)
        logits = jnp.where(mine, logits, LOW)
        top = jnp.max(logits, axis=-1, keepdims=True)
        e = jnp.exp(logits - top)
        probs = (e / jnp.sum(e, axis=-1, keepdims=True)).astype(BF)
        mixed = mixed + jnp.dot(probs, v_h, preferred_element_type=F32)
    result = x + jnp.dot(mixed.astype(BF), w_out[...], preferred_element_type=F32)
    encoded[...] = result.astype(BF).reshape(GROUPS, 2, NT, E)
    c = got[:, :, E:].astype(F32)
    c = c + pltpu.roll(c, 127, 2)
    hi, lo = best_two(c, pltpu.roll(c, 126, 2))
    line = lax.broadcasted_iota(jnp.int32, (16, 128), 0)
    lane = lax.broadcasted_iota(jnp.int32, (16, 128), 1)
    for k, value in enumerate((hi[0], lo[0])):
        turned = jnp.where(line == lane, value[:, 0:1], 0.0) + jnp.where(line + 16 == lane, value[:, 4:5], 0.0)
        best[k : k + 1, :] = jnp.sum(turned, axis=0, keepdims=True)[:, :GROUPS]


def vmem(count):
    return [pl.BlockSpec(memory_space=pltpu.VMEM)] * count


def ring_moved(piece, crossed=0):
    pairs = []
    for at in range(RING):
        pairs.append((2 * at + crossed, 2 * ((at + 1) % RING)))
        pairs.append((2 * at + 1 - crossed, 2 * ((at - 1) % RING) + 1))
    return lax.ppermute(piece, ("zh", "core"), pairs)


def pack_kernel(y, ids, slab, w_query, w_key, w_value, w_out, pair, packed, held):
    rows = pl.ds(pl.multiple_of(y[0] * SLAB_ROWS, 8), SLAB_ROWS)
    held[...] = jnp.zeros_like(held)
    held[:SLAB_ROWS, :] = slab[rows, :]
    flat = ids[...].astype(F32)
    owner = jnp.floor((flat + 0.5) * (1.0 / ROWS))
    held[SLAB_ROWS : SLAB_ROWS + 2, :GROUPS] = owner
    held[SLAB_ROWS + 2 : SLAB_ROWS + 4, :GROUPS] = flat - owner * ROWS
    pair[...] = held[...].astype(BF)
    part = w_query.shape[0]
    half = part // 2
    packed[:part, :HD] = w_query[...]
    packed[:part, HD:] = w_key[...]
    packed[part : part + half, :HD] = w_value[:half, :]
    packed[part : part + half, HD:] = w_value[half:, :]
    packed[part + half :, :] = w_out[...]


def project_kernel(acts, whole, keyed, valued, w_query, w_out, w_key, w_value):
    part = E // 4
    half = part // 2
    for b in range(4):
        at = b * part
        w_query[at : at + part, :] = whole[b, :part, :HD]
        w_key[at : at + part, :] = whole[b, :part, HD:]
        w_value[at : at + half, :] = whole[b, part : part + half, :HD]
        w_value[at + half : at + part, :] = whole[b, part : part + half, HD:]
        w_out[b * half : (b + 1) * half, :] = whole[b, part + half :, :]
    x = acts[...]
    keyed[...] = jnp.dot(x, w_key[...], preferred_element_type=F32).astype(BF)
    valued[...] = jnp.dot(x, w_value[...], preferred_element_type=F32).astype(BF)


def marks_of(owner, local, zh, parity):
    at = lax.iota(jnp.int32, PAIRS)
    rank = jnp.max(
        jnp.where((owner[:, None] == owner[None, :]) & (at[:, None] > at[None, :]), 1, 0), axis=1
    )
    core = owner & 1
    away = (zh - (owner >> 2)) & 7
    direct = (away & 3) == 0
    server = jnp.where(direct, core, away >> 2)
    steps = jnp.where(away > 4, 8 - away, away)
    slot = jnp.where(direct, 12 + (away >> 1), (steps - 1) * 4 + (core ^ server) * 2) + rank
    code = ((owner >> 1) & 1) * 128 + (((owner >> 5) << 1) | server) * SLOTS + slot
    label = lax.iota(jnp.int32, 128) + parity * 128
    marks = jnp.sum(jnp.where(code[None, :] == label[:, None], local[None, :] + 1, 0), axis=1)
    return code, marks.astype(BF)


def per_device(keys, slab, neighbour_ids, group_acts, table, norm_gain, w_query, w_key, w_value, w_out):
    y = lax.axis_index("pb")
    zh = lax.axis_index("zh")
    zl = lax.axis_index("zl")
    flat = neighbour_ids.T.reshape(PAIRS)
    owner = lax.div(flat, ROWS)
    local = flat - owner * ROWS
    mine, packed = pl.pallas_call(
        pack_kernel,
        out_shape=(
            jax.ShapeDtypeStruct((KEYPAD, KEY), BF),
            jax.ShapeDtypeStruct((2 * w_query.shape[0], E), BF),
        ),
        in_specs=[pl.BlockSpec(memory_space=pltpu.SMEM), *vmem(6)],
        out_specs=tuple(vmem(2)),
        scratch_shapes=[pltpu.VMEM((KEYPAD, KEY), F32)],
    )(y.reshape(1).astype(jnp.int32), neighbour_ids.T, slab, w_query, w_key, w_value, w_out)
    quarter = mine[:SLAB_ROWS]
    pair = lax.ppermute(mine, "zl", [(0, 1), (1, 0)])
    token = lax.dynamic_index_in_dim(table, y, axis=1, keepdims=False)
    both = jnp.concatenate([quarter, pair[:SLAB_ROWS]], axis=1)
    both = jnp.pad(both, ((0, 0), (0, E - 2 * KEY)))
    piece = jnp.concatenate([token, both], axis=0)
    ours = [piece]
    others = [piece]
    for k in range(3):
        ours.append(ring_moved(ours[-1]))
        others.append(ring_moved(others[-1], crossed=1 if k == 0 else 0))
    far = ring_moved(ours[3])
    pieces = [ours[1], others[1], ours[2], others[2], ours[3], others[3], ours[0], far]
    whole = lax.all_gather(packed, "pb", axis=0, tiled=False)
    code, own = marks_of(owner, local, zh, zl)
    partner = pair[SLAB_ROWS : SLAB_ROWS + 4, :GROUPS].astype(jnp.int32)
    _, other = marks_of(partner[:2].reshape(PAIRS), partner[2:].reshape(PAIRS), zh, zl)
    place = (code >> 7) * (PLANE * SLOTS) + (code & 127)
    place = place.reshape(2, GROUPS).T.reshape(GROUPS, 2, 1) + lax.iota(jnp.int32, NT) * 128
    place = place.reshape(PAIRS * NT, 1)
    sent = jnp.pad(keys.astype(BF), ((0, KEYPAD - GROUPS), (0, 0)))
    asks = jnp.stack([own.reshape(8, SLOTS), other.reshape(8, SLOTS)], axis=1)
    asks = jnp.pad(asks, ((0, 0), (GROUPS, KEYPAD - GROUPS - 2), (0, KEY - SLOTS)))
    sent = sent[None] + asks
    sent = jnp.broadcast_to(sent[None], (4, 8, KEYPAD, KEY)).reshape(PLANE, KEYPAD, KEY)
    asked = lax.all_to_all(sent, FLAT, split_axis=0, concat_axis=0, tiled=True)
    wanted = asked[:, GROUPS : GROUPS + 2, :SLOTS].astype(jnp.int32)
    wanted = jnp.where(zl == 0, jnp.stack([wanted[:, 0], wanted[:, 1]]), jnp.stack([wanted[:, 1], wanted[:, 0]]))
    block = lax.iota(jnp.int32, SLOTS) // 2
    wanted = jnp.where(wanted > 0, block * ROWS + wanted - 1, -1).reshape(SERVERS * SLOTS, 1)
    parity = jnp.full((1, 1, 128), zl, jnp.int32)
    served = pl.pallas_call(
        serve_kernel,
        out_shape=jax.ShapeDtypeStruct((SERVERS, SLOTS, WIDE), BF),
        in_specs=vmem(3 + RING),
        out_specs=pl.BlockSpec(memory_space=pltpu.HBM),
        scratch_shapes=[
            pltpu.VMEM((RING * ROWS, E), BF),
            pltpu.VMEM((RING * 2 * SLAB_ROWS, KEY), F32),
            pltpu.VMEM((SERVERS, SLOTS, WIDE), BF),
            pltpu.SemaphoreType.DMA((4,)),
        ],
        compiler_params=pltpu.CompilerParams(vmem_limit_bytes=SERVE_LIMIT),
    )(parity, wanted, asked, *pieces)
    served, whole = lax.optimization_barrier((served, whole))
    got = lax.all_to_all(served, NEAR, split_axis=0, concat_axis=0, tiled=True)
    keyed, valued, w_q, w_o = pl.pallas_call(
        project_kernel,
        out_shape=(
            jax.ShapeDtypeStruct((GROUPS * CT, HD), BF),
            jax.ShapeDtypeStruct((GROUPS * CT, HD), BF),
            jax.ShapeDtypeStruct((E, HD), BF),
            jax.ShapeDtypeStruct((HD, E), BF),
        ),
        in_specs=vmem(2),
        out_specs=tuple(vmem(4)),
        scratch_shapes=[pltpu.VMEM((E, HD), BF), pltpu.VMEM((E, HD), BF)],
        compiler_params=pltpu.CompilerParams(vmem_limit_bytes=LIMIT),
    )(group_acts.reshape(GROUPS * CT, E), whole)
    best, encoded = pl.pallas_call(
        layer_kernel,
        out_shape=(
            jax.ShapeDtypeStruct((2, GROUPS), F32),
            jax.ShapeDtypeStruct((GROUPS, 2, NT, E), BF),
        ),
        in_specs=vmem(7),
        out_specs=tuple(vmem(2)),
        compiler_params=pltpu.CompilerParams(vmem_limit_bytes=LAYER_LIMIT),
    )(place, got, keyed, valued, w_q, w_o, norm_gain.reshape(1, E))
    return best.T, encoded


def solution(mesh):
    split = Mesh(mesh.devices.reshape(4, RING, 2, 2, 4), SPLIT)
    return jax.shard_map(
        per_device,
        mesh=split,
        in_specs=(
            P(SPLIT, None),
            P(DB, None),
            P(SPLIT, None),
            P(SPLIT, None, None),
            P(DB, None, None),
            P(),
            P("pb", None),
            P("pb", None),
            P("pb", None),
            P("pb", None),
        ),
        out_specs=(P(SPLIT, None), P(SPLIT, None, None, None)),
        check_vma=False,
    )
```

```python
import jax
import jax.numpy as jnp
from jax import lax
from jax.experimental import pallas as pl
from jax.experimental.pallas import tpu as pltpu
from jax.sharding import Mesh
from jax.sharding import PartitionSpec as P

KEY = 384
E = 896
HEADS = 7
HSIZE = 64
HD = HEADS * HSIZE
NT = 4
CT = 4
ROWS = 96
GROUPS = 26
PAIRS = 2 * GROUPS
RING = 8
SLAB_ROWS = 24
PIECE = ROWS + SLAB_ROWS
PLANE = 32
SERVERS = 2 * PLANE
SLOTS = 16
KEYPAD = 32
WIDE = E + 128
LIMIT = 24 * 2**20
LAYER_LIMIT = 50 * 2**20
SERVE_LIMIT = 52 * 2**20
LOW = -1.0e38
SPLIT = ("x", "zh", "zl", "core", "pb")
DB = ("x", "zh", "zl", "core")
FLAT = ("pb", "x", "core")
NEAR = ("zl", *FLAT)
BF = jnp.bfloat16
F32 = jnp.float32


def best_two(hi, lo):
    count = hi.shape[0]
    while count > 1:
        half = count // 2
        h1, h2, l1, l2 = hi[:half], hi[half:count], lo[:half], lo[half:count]
        hi, lo = jnp.maximum(h1, h2), jnp.maximum(jnp.minimum(h1, h2), jnp.maximum(l1, l2))
        count = half
    return hi, lo


def serve_kernel(parity, code, keys, *refs):
    *pieces, sent, held, slab, out, sems = refs
    for k, piece in enumerate(pieces):
        held[k * ROWS : (k + 1) * ROWS, :] = piece[:ROWS, :]
        extra = piece[ROWS:, :]
        for part in range(2):
            at = (2 * k + part) * SLAB_ROWS
            slab[at : at + SLAB_ROWS, :] = extra[:, part * KEY : (part + 1) * KEY].astype(F32)
    step = 256
    n = step // SLOTS
    copies = []
    for i in range(SERVERS * SLOTS // step):
        label = lax.broadcasted_iota(jnp.int32, (step, RING * ROWS), 1)
        pick = (code[i * step : (i + 1) * step, :] == label).astype(F32).astype(BF)
        found = jnp.dot(pick, held[...], preferred_element_type=F32).astype(BF)
        out[i * n : (i + 1) * n, :, :E] = found.reshape(n, SLOTS, E)
        block = pl.ds(i * n, n)
        copies.append(pltpu.make_async_copy(out.at[block, :, pl.ds(0, E)], sent.at[block, :, pl.ds(0, E)], sems.at[i]))
        copies[-1].start()
    wide = 512
    n = wide // KEYPAD
    rows = slab[...].astype(BF)
    mine = parity[...]
    for i in range(PLANE * KEYPAD // wide):
        block = keys[i * n : (i + 1) * n].reshape(wide, KEY)
        rating = lax.dot_general(
            rows, block, (((1,), (1,)), ((), ())), preferred_element_type=F32
        ) * (KEY**-0.5)
        h1, h2, h3 = rating[:128], rating[128:256], rating[256:]
        hi, lo = jnp.maximum(h1, h2), jnp.minimum(h1, h2)
        hi, lo = jnp.maximum(hi, h3), jnp.maximum(lo, jnp.minimum(hi, h3))
        hi, lo = best_two(hi, lo)
        hi_a = hi.astype(BF).astype(F32)
        lo_a = lo.astype(BF).astype(F32)
        line = lax.broadcasted_iota(jnp.int32, (16, wide), 0)
        parts = jnp.where(
            line == 0,
            hi_a,
            jnp.where(line == 1, hi - hi_a, jnp.where(line == 2, lo_a, jnp.where(line == 3, lo - lo_a, 0.0))),
        ).astype(BF)
        for half in range(2):
            unit = (
                lax.broadcasted_iota(jnp.int32, (16, 128), 0) + 4 * half
                == lax.broadcasted_iota(jnp.int32, (16, 128), 1)
            ).astype(F32).astype(BF)
            turned = lax.dot_general(
                parts, unit, (((0,), (0,)), ((), ())), preferred_element_type=F32
            ).reshape(n, 2, 16, 128)
            if half == 0:
                total = turned[:, 0]
            else:
                total = total + turned[:, 1]
        lane = lax.broadcasted_iota(jnp.int32, (1, 1, 128), 2)
        none = jnp.where(lax.rem(lane, 2) == 0, LOW, 0.0)
        for z in range(2):
            at = z * PLANE + i * n
            out[at : at + n, :, E:] = jnp.where(mine == z, total, none).astype(BF)
    lanes = pl.ds(E, WIDE - E)
    copies.append(pltpu.make_async_copy(out.at[:, :, lanes], sent.at[:, :, lanes], sems.at[4]))
    copies[-1].start()
    for copy in copies:
        copy.wait()


def layer_kernel(place, got, keyed, valued, w_query, w_out, gain, best, encoded):
    label = lax.broadcasted_iota(jnp.int32, (PAIRS * NT, SERVERS * SLOTS), 1)
    pick = (place[...] == label).astype(F32).astype(BF)
    rows = got[:, :, :E].reshape(SERVERS * SLOTS, E)
    x = jnp.dot(pick, rows, preferred_element_type=F32)
    square = jnp.mean(x * x, axis=-1, keepdims=True)
    normed = (x * lax.rsqrt(square + 1e-06) * gain[...]).astype(BF)
    query = jnp.dot(normed, w_query[...], preferred_element_type=F32).astype(BF)
    query = query.astype(F32)
    k_all = keyed[...]
    v_all = valued[...].astype(F32)
    head = lax.broadcasted_iota(jnp.int32, (1, HD), 1) // HSIZE
    mine = (
        lax.broadcasted_iota(jnp.int32, (PAIRS * NT, GROUPS * CT), 0) // (2 * NT)
        == lax.broadcasted_iota(jnp.int32, (PAIRS * NT, GROUPS * CT), 1) // CT
    )
    mixed = jnp.zeros((PAIRS * NT, HD), F32)
    for h in range(HEADS):
        q_h = jnp.where(head == h, query, 0.0).astype(BF)
        v_h = jnp.where(head == h, v_all, 0.0).astype(BF)
        logits = lax.dot_general(
            q_h, k_all, (((1,), (1,)), ((), ())), preferred_element_type=F32
        ) * (HSIZE**-0.5)
        logits = jnp.where(mine, logits, LOW)
        top = jnp.max(logits, axis=-1, keepdims=True)
        e = jnp.exp(logits - top)
        probs = (e / jnp.sum(e, axis=-1, keepdims=True)).astype(BF)
        mixed = mixed + jnp.dot(probs, v_h, preferred_element_type=F32)
    result = x + jnp.dot(mixed.astype(BF), w_out[...], preferred_element_type=F32)
    encoded[...] = result.astype(BF).reshape(GROUPS, 2, NT, E)
    c = got[:, :, E:].astype(F32)
    c = c + pltpu.roll(c, 127, 2)
    hi, lo = best_two(c, pltpu.roll(c, 126, 2))
    line = lax.broadcasted_iota(jnp.int32, (16, 128), 0)
    lane = lax.broadcasted_iota(jnp.int32, (16, 128), 1)
    for k, value in enumerate((hi[0], lo[0])):
        turned = jnp.where(line == lane, value[:, 0:1], 0.0) + jnp.where(line + 16 == lane, value[:, 4:5], 0.0)
        best[k : k + 1, :] = jnp.sum(turned, axis=0, keepdims=True)[:, :GROUPS]


def vmem(count):
    return [pl.BlockSpec(memory_space=pltpu.VMEM)] * count


def ring_moved(piece, crossed=0):
    pairs = []
    for at in range(RING):
        pairs.append((2 * at + crossed, 2 * ((at + 1) % RING)))
        pairs.append((2 * at + 1 - crossed, 2 * ((at - 1) % RING) + 1))
    return lax.ppermute(piece, ("zh", "core"), pairs)


def pack_kernel(y, ids, slab, w_query, w_key, w_value, w_out, pair, packed, held):
    rows = pl.ds(pl.multiple_of(y[0] * SLAB_ROWS, 8), SLAB_ROWS)
    held[...] = jnp.zeros_like(held)
    held[:SLAB_ROWS, :] = slab[rows, :]
    flat = ids[...].astype(F32)
    owner = jnp.floor((flat + 0.5) * (1.0 / ROWS))
    held[SLAB_ROWS : SLAB_ROWS + 2, :GROUPS] = owner
    held[SLAB_ROWS + 2 : SLAB_ROWS + 4, :GROUPS] = flat - owner * ROWS
    pair[...] = held[...].astype(BF)
    part = w_query.shape[0]
    half = part // 2
    packed[:part, :HD] = w_query[...]
    packed[:part, HD:] = w_key[...]
    packed[part : part + half, :HD] = w_value[:half, :]
    packed[part : part + half, HD:] = w_value[half:, :]
    packed[part + half :, :] = w_out[...]


def project_kernel(acts, whole, keyed, valued, w_query, w_out, w_key, w_value):
    part = E // 4
    half = part // 2
    for b in range(4):
        at = b * part
        w_query[at : at + part, :] = whole[b, :part, :HD]
        w_key[at : at + part, :] = whole[b, :part, HD:]
        w_value[at : at + half, :] = whole[b, part : part + half, :HD]
        w_value[at + half : at + part, :] = whole[b, part : part + half, HD:]
        w_out[b * half : (b + 1) * half, :] = whole[b, part + half :, :]
    x = acts[...]
    keyed[...] = jnp.dot(x, w_key[...], preferred_element_type=F32).astype(BF)
    valued[...] = jnp.dot(x, w_value[...], preferred_element_type=F32).astype(BF)


def marks_of(owner, local, zh, parity):
    at = lax.iota(jnp.int32, PAIRS)
    rank = jnp.max(
        jnp.where((owner[:, None] == owner[None, :]) & (at[:, None] > at[None, :]), 1, 0), axis=1
    )
    core = owner & 1
    away = (zh - (owner >> 2)) & 7
    direct = (away & 3) == 0
    server = jnp.where(direct, core, away >> 2)
    steps = jnp.where(away > 4, 8 - away, away)
    slot = jnp.where(direct, 12 + (away >> 1), (steps - 1) * 4 + (core ^ server) * 2) + rank
    code = ((owner >> 1) & 1) * 128 + (((owner >> 5) << 1) | server) * SLOTS + slot
    label = lax.iota(jnp.int32, 128) + parity * 128
    marks = jnp.sum(jnp.where(code[None, :] == label[:, None], local[None, :] + 1, 0), axis=1)
    return code, marks.astype(BF)


def per_device(keys, slab, neighbour_ids, group_acts, table, norm_gain, w_query, w_key, w_value, w_out):
    y = lax.axis_index("pb")
    zh = lax.axis_index("zh")
    zl = lax.axis_index("zl")
    flat = neighbour_ids.T.reshape(PAIRS)
    owner = lax.div(flat, ROWS)
    local = flat - owner * ROWS
    mine, packed = pl.pallas_call(
        pack_kernel,
        out_shape=(
            jax.ShapeDtypeStruct((KEYPAD, KEY), BF),
            jax.ShapeDtypeStruct((2 * w_query.shape[0], E), BF),
        ),
        in_specs=[pl.BlockSpec(memory_space=pltpu.SMEM), *vmem(6)],
        out_specs=tuple(vmem(2)),
        scratch_shapes=[pltpu.VMEM((KEYPAD, KEY), F32)],
    )(y.reshape(1).astype(jnp.int32), neighbour_ids.T, slab, w_query, w_key, w_value, w_out)
    quarter = mine[:SLAB_ROWS]
    pair = lax.ppermute(mine, "zl", [(0, 1), (1, 0)])
    token = lax.dynamic_index_in_dim(table, y, axis=1, keepdims=False)
    both = jnp.concatenate([quarter, pair[:SLAB_ROWS]], axis=1)
    both = jnp.pad(both, ((0, 0), (0, E - 2 * KEY)))
    piece = jnp.concatenate([token, both], axis=0)
    ours = [piece]
    others = [piece]
    for k in range(3):
        ours.append(ring_moved(ours[-1]))
        others.append(ring_moved(others[-1], crossed=1 if k == 0 else 0))
    far = ring_moved(ours[3])
    pieces = [ours[1], others[1], ours[2], others[2], ours[3], others[3], ours[0], far]
    whole = lax.all_gather(packed, "pb", axis=0, tiled=False)
    code, own = marks_of(owner, local, zh, zl)
    partner = pair[SLAB_ROWS : SLAB_ROWS + 4, :GROUPS].astype(jnp.int32)
    _, other = marks_of(partner[:2].reshape(PAIRS), partner[2:].reshape(PAIRS), zh, zl)
    place = (code >> 7) * (PLANE * SLOTS) + (code & 127)
    place = place.reshape(2, GROUPS).T.reshape(GROUPS, 2, 1) + lax.iota(jnp.int32, NT) * 128
    place = place.reshape(PAIRS * NT, 1)
    sent = jnp.pad(keys.astype(BF), ((0, KEYPAD - GROUPS), (0, 0)))
    asks = jnp.stack([own.reshape(8, SLOTS), other.reshape(8, SLOTS)], axis=1)
    asks = jnp.pad(asks, ((0, 0), (GROUPS, KEYPAD - GROUPS - 2), (0, KEY - SLOTS)))
    sent = sent[None] + asks
    sent = jnp.broadcast_to(sent[None], (4, 8, KEYPAD, KEY)).reshape(PLANE, KEYPAD, KEY)
    asked = lax.all_to_all(sent, FLAT, split_axis=0, concat_axis=0, tiled=True)
    wanted = asked[:, GROUPS : GROUPS + 2, :SLOTS].astype(jnp.int32)
    wanted = jnp.where(zl == 0, jnp.stack([wanted[:, 0], wanted[:, 1]]), jnp.stack([wanted[:, 1], wanted[:, 0]]))
    block = lax.iota(jnp.int32, SLOTS) // 2
    wanted = jnp.where(wanted > 0, block * ROWS + wanted - 1, -1).reshape(SERVERS * SLOTS, 1)
    parity = jnp.full((1, 1, 128), zl, jnp.int32)
    served = pl.pallas_call(
        serve_kernel,
        out_shape=jax.ShapeDtypeStruct((SERVERS, SLOTS, WIDE), BF),
        in_specs=vmem(3 + RING),
        out_specs=pl.BlockSpec(memory_space=pltpu.HBM),
        scratch_shapes=[
            pltpu.VMEM((RING * ROWS, E), BF),
            pltpu.VMEM((RING * 2 * SLAB_ROWS, KEY), F32),
            pltpu.VMEM((SERVERS, SLOTS, WIDE), BF),
            pltpu.SemaphoreType.DMA((5,)),
        ],
        compiler_params=pltpu.CompilerParams(vmem_limit_bytes=SERVE_LIMIT),
    )(parity, wanted, asked, *pieces)
    served, whole = lax.optimization_barrier((served, whole))
    got = lax.all_to_all(served, NEAR, split_axis=0, concat_axis=0, tiled=True)
    keyed, valued, w_q, w_o = pl.pallas_call(
        project_kernel,
        out_shape=(
            jax.ShapeDtypeStruct((GROUPS * CT, HD), BF),
            jax.ShapeDtypeStruct((GROUPS * CT, HD), BF),
            jax.ShapeDtypeStruct((E, HD), BF),
            jax.ShapeDtypeStruct((HD, E), BF),
        ),
        in_specs=vmem(2),
        out_specs=tuple(vmem(4)),
        scratch_shapes=[pltpu.VMEM((E, HD), BF), pltpu.VMEM((E, HD), BF)],
        compiler_params=pltpu.CompilerParams(vmem_limit_bytes=LIMIT),
    )(group_acts.reshape(GROUPS * CT, E), whole)
    best, encoded = pl.pallas_call(
        layer_kernel,
        out_shape=(
            jax.ShapeDtypeStruct((2, GROUPS), F32),
            jax.ShapeDtypeStruct((GROUPS, 2, NT, E), BF),
        ),
        in_specs=vmem(7),
        out_specs=tuple(vmem(2)),
        compiler_params=pltpu.CompilerParams(vmem_limit_bytes=LAYER_LIMIT),
    )(place, got, keyed, valued, w_q, w_o, norm_gain.reshape(1, E))
    return best.T, encoded


def solution(mesh):
    split = Mesh(mesh.devices.reshape(4, RING, 2, 2, 4), SPLIT)
    return jax.shard_map(
        per_device,
        mesh=split,
        in_specs=(
            P(SPLIT, None),
            P(DB, None),
            P(SPLIT, None),
            P(SPLIT, None, None),
            P(DB, None, None),
            P(),
            P("pb", None),
            P("pb", None),
            P("pb", None),
            P("pb", None),
        ),
        out_specs=(P(SPLIT, None), P(SPLIT, None, None, None)),
        check_vma=False,
    )
```
